256 devices in a mesh: dp: 128 (over z, x_lo, y, core), mp: 2 (over x_hi).
Axes of the slice: x: 4 (x_hi: 2, x_lo: 2; x = x_hi * 2 + x_lo), y: 4, z: 8, core: 2. Of those that a mesh axis runs over, the one named last changes fastest.
Arguments:
- tokens: bfloat16 [131072, 1024], P('dp', 'mp'), may hold values from -6 to 6
- norm_gain: float32 [1024], replicated, may hold values from 0.25 to 1.75
- fc_in: bfloat16 [1024, 4096], P(None, 'mp'), may hold values from -0.1875 to 0.1875
- fc_out: bfloat16 [4096, 1024], P('mp'), may hold values from -0.09375 to 0.09375
- projection: bfloat16 [1024, 1024], P(None, 'mp'), may hold values from -0.1875 to 0.1875
- slots: int32 [128, 1024], P('dp'), may hold values from 0 to 31, never falling along the last dimension, each value on 1 to 64 neighbouring positions
- images: bfloat16 [32768, 1024], P(('dp', 'mp')), may hold values from -6 to 6
- labels: int32 [32768], P(('dp', 'mp')), may hold values from 0 to 4095
- logit_scale: float32 [1], replicated, may hold values from 5 to 15
- logit_bias: float32 [1], replicated, may hold values from -12 to -4
Outputs:
- text_embedding: bfloat16 [4096, 1024], P('dp', 'mp')
- grad_image: float32 [32768, 1024], P(('dp', 'mp'))
- grad_text: float32 [4096, 1024], P('dp', 'mp')
The draws below stay inside these ranges and needn't reach their ends.
Inputs may be any that keep to these rules, and one draw needn't show every extreme that they name: Within each row the slot numbers never fall; every one of the 32 slots has 1 to 64 tokens, and some slot has exactly 64.
All inputs are finite; a program needn't handle non-finite values.
Results may differ from the reference program's by a relative error of at most 0.0053.
Values may be sent and summed in bfloat16 or wider, within the bound.
No kernel may reach another device: no remote copies, remote signals or barrier semaphores. Data moves between devices by JAX's collectives and lax.ppermute only.
A program may use at most 128 MiB of HBM per device.

```python
import math
import jax
import jax.numpy as jnp
import numpy as np
from jax import lax

D = 1024
FF = 4096
E = 1024
MAXLEN = 64
CAP_DEV = 32
TOK_DEV = 1024
GROUPS = 128
TEXTS = 4096
TOKENS = 131072
IMAGES = 32768
N_DP = 128


def plant(values, own_key, smallest, top_value):
    extent = values.shape
    index_at = [jax.random.randint(jax.random.fold_in(own_key, axis), (), 0, extent[axis]) for axis in range(len(extent))]
    values = values.at[tuple(index_at)].set(smallest)
    longest = extent.index(max(extent))
    index_at[longest] = (index_at[longest] + 1) % extent[longest]
    return values.at[tuple(index_at)].set(top_value)


def shard_levels(key, shape, split, low, largest):
    def one(dim, shards_of):
        steps = jax.random.uniform(jax.random.fold_in(jax.random.fold_in(key, 6), dim), (shards_of,), jnp.float32, low / len(split), largest / len(split))
        return jnp.repeat(jnp.exp(steps), shape[dim] // shards_of).reshape((-1,) + (1,) * (len(shape) - dim - 1))

    loudness = one(*split[0])
    for cut in split[1:]:
        loudness = loudness * one(*cut)
    return loudness


def split_up(number_of, total, limit, skew):
    weights = [(1 << 20) // math.isqrt(standing ** skew) + 1 for standing in range(2, number_of + 1)]
    rest, given = total - limit - (number_of - 1), [1] * (number_of - 1)
    while rest > 0:
        candidates = [i for i in range(number_of - 1) if given[i] < limit]
        mass, budget = sum([weights[i] for i in candidates]), rest
        for i in candidates:
            addition = min(limit - given[i], max(1, budget * weights[i] // mass), rest)
            given[i] = given[i] + addition
            rest = rest - addition
    return np.array([limit] + given)


def ragged(own_key, count, total, most, lean):
    if count == 2:
        one = jax.random.randint(own_key, (), max(1, total - most), min(most, total - 1) + 1)
        return jnp.stack([one, total - one])
    tallies = jnp.asarray(split_up(count, total, most, lean), jnp.int32)
    couples = (count - 1) // 2
    donor, taker = tallies[1:1 + 2 * couples:2], tallies[2:2 + 2 * couples:2]
    room = jnp.minimum(donor - 1, most - taker)
    shifted = jax.random.randint(jax.random.fold_in(own_key, 1), (couples,), 0, 1 << 20) % (room + 1)
    tallies = tallies.at[1:1 + 2 * couples:2].set(donor - shifted).at[2:2 + 2 * couples:2].set(taker + shifted)
    return tallies[jax.random.permutation(jax.random.fold_in(own_key, 2), count)]


def normal_values(stream_key, shape, scale, reach, pieces=(), kind=jnp.bfloat16):
    factor_of = shard_levels(stream_key, shape, pieces, -0.22, 0.18) if pieces else 1.0
    drawn = jax.random.normal(stream_key, shape, jnp.float32) * scale * factor_of
    return jnp.minimum(jnp.maximum(drawn, -reach), reach).astype(kind)


def setup_inputs(seed: int = 0) -> dict:
    key_of = jax.random.split(jax.random.key(seed), 11)
    tokens = normal_values(key_of[0], (TOKENS, D), 1.0, 6.0, ((0, 128), (1, 2)))
    norm_gain = jnp.clip(1.0 + 0.15 * jax.random.normal(key_of[1], (D,), jnp.float32), 0.25, 1.75)
    fc_in = normal_values(key_of[2], (D, FF), D ** -0.5, 0.1875, ((1, 2),))
    fc_out = normal_values(key_of[3], (FF, D), FF ** -0.5, 0.09375, ((0, 2),))
    projection = normal_values(key_of[4], (D, E), D ** -0.5, 0.1875, ((1, 2),))
    slots = jax.vmap(lambda own: jnp.searchsorted(jnp.cumsum(ragged(own, CAP_DEV, TOK_DEV, MAXLEN, 1)), jnp.arange(TOK_DEV), side="right"))(jax.random.split(key_of[5], GROUPS)).reshape((GROUPS, TOK_DEV)).astype(jnp.int32)
    images = normal_values(key_of[6], (IMAGES, E), 1.0, 6.0, ((0, 256),))
    labels = plant(jax.random.randint(key_of[7], (IMAGES,), 0, TEXTS), jax.random.fold_in(key_of[7], 1), 0, TEXTS - 1).astype(jnp.int32)
    logit_scale = jnp.clip(jax.random.uniform(key_of[8], (1,), jnp.float32, 5.0, 15.0), 5.0, 15.0)
    logit_bias = jnp.clip(jax.random.uniform(key_of[9], (1,), jnp.float32, -12.0, -4.0), -12.0, -4.0)
    return {"tokens": tokens, "norm_gain": norm_gain, "fc_in": fc_in, "fc_out": fc_out, "projection": projection, "slots": slots, "images": images, "labels": labels, "logit_scale": logit_scale, "logit_bias": logit_bias}


def reference(tokens, norm_gain, fc_in, fc_out, projection, slots, images, labels, logit_scale, logit_bias):
    states = tokens.astype(jnp.float32)
    center = states - lax.optimization_barrier(jnp.mean(states, axis=1, keepdims=True))
    spread = lax.optimization_barrier(jnp.mean(center * center, axis=1, keepdims=True))
    normed = (center * lax.rsqrt(spread + 1e-06) * norm_gain[None, :]).astype(jnp.bfloat16)
    hidden = jax.nn.gelu(jnp.dot(normed, fc_in, preferred_element_type=jnp.float32), approximate=True).astype(jnp.bfloat16)
    resid = states + jnp.dot(hidden, fc_out, preferred_element_type=jnp.float32)
    offsets = (jnp.arange(GROUPS, dtype=jnp.int32) * CAP_DEV)[:, None]
    caption_ids = (slots.astype(jnp.int32) + offsets).reshape(-1).astype(jnp.int32)
    sums = jax.ops.segment_sum(resid, caption_ids, num_segments=TEXTS)
    counts = jax.ops.segment_sum(jnp.ones((TOKENS,), jnp.float32), caption_ids, num_segments=TEXTS)
    pooled = (sums / counts[:, None]).astype(jnp.bfloat16)
    emb = jnp.dot(pooled, projection, preferred_element_type=jnp.float32)
    text_embedding = (emb * lax.rsqrt(lax.optimization_barrier(jnp.sum(emb * emb, axis=1, keepdims=True)) + 1e-06)).astype(jnp.bfloat16)
    imgs = images.astype(jnp.float32)
    img = (imgs * lax.rsqrt(lax.optimization_barrier(jnp.sum(imgs * imgs, axis=1, keepdims=True)) + 1e-06)).astype(jnp.bfloat16)
    scale = logit_scale[0]
    bias = logit_bias[0]
    columns = jnp.arange(TEXTS, dtype=jnp.int32)
    block_rows = IMAGES // N_DP
    img_blocks = img.reshape(N_DP, block_rows, E)
    label_blocks = labels.reshape(N_DP, block_rows)

    def one_block(total, inputs):
        block, marks = inputs
        logit = scale * jnp.dot(block, text_embedding.T, preferred_element_type=jnp.float32) + bias
        sign = jnp.where(marks[:, None] == columns[None, :], 1.0, -1.0).astype(jnp.float32)
        weight = (-scale * sign * jax.nn.sigmoid(-sign * logit)).astype(jnp.bfloat16)
        grad_block = jnp.dot(weight, text_embedding, preferred_element_type=jnp.float32)
        total = total + jnp.dot(weight.T, block, preferred_element_type=jnp.float32)
        return (total, grad_block)
    start = jnp.zeros((TEXTS, E), jnp.float32)
    grad_text, grad_blocks = lax.scan(one_block, start, (img_blocks, label_blocks))
    grad_image = grad_blocks.reshape(IMAGES, E)
    return (text_embedding, grad_image, grad_text)
```

```python
import functools
import jax
import jax.numpy as jnp
from jax import lax
from jax.experimental import pallas as pl
from jax.experimental.pallas import tpu as pltpu
from jax.sharding import Mesh, PartitionSpec as P

CAP_DEV = 32
CHUNKS = 4
FF_TILE = 512
IMG_TILE = 256
IMG_ROWS = 128
PAD = 128
AXES = ("zh", "zl", "xl", "y", "core", "xh")
SIZES = (4, 2, 2, 4, 2, 2)
DP = ("zh", "zl", "xl", "y", "core")
MP = "xh"
BF = jnp.bfloat16
F32 = jnp.float32
SWAP = [(0, 1), (1, 0)]
SMALL = pl.CostEstimate(flops=1000, bytes_accessed=1000, transcendentals=0)


def dot(a, b):
    return jnp.dot(a, b, preferred_element_type=F32)


def shift(n, k):
    return [(i, (i + k) % n) for i in range(n)]


def ring_x(k):
    place = lambda x: (x % 2) * 2 + x // 2
    return [(place(x), place((x + k) % 4)) for x in range(4)]


def mlp_kernel(last, low, slot, own, other, gain, w_in, *refs):
    if last:
        w_out, hid_in, st_in, out, st_out, normed, acc = refs
    else:
        hid_in, st_in, hid_out, st_out, normed = refs
    step = pl.program_id(0)
    half = own.shape[1]
    captions = lax.broadcasted_iota(jnp.int32, (CAP_DEV, own.shape[0]), 0)
    members = (captions == slot[...]).astype(F32).astype(BF)

    @pl.when(step == 0)
    def _():
        is_low = low[0] == 1
        mine = own[...].astype(F32)
        theirs = other[...].astype(F32)
        lo = jnp.where(is_low, mine, theirs)
        hi = jnp.where(is_low, theirs, mine)
        size = 1.0 / (2 * half)
        mean = (jnp.sum(lo, axis=1, keepdims=True) + jnp.sum(hi, axis=1, keepdims=True)) * size
        st_out[:, :half] = st_in[:, :half] + dot(members, lo.astype(BF))
        st_out[:, half:] = st_in[:, half:] + dot(members, hi.astype(BF))
        lo = lo - mean
        hi = hi - mean
        spread = (
            jnp.sum(lo * lo, axis=1, keepdims=True) + jnp.sum(hi * hi, axis=1, keepdims=True)
        ) * size
        inverse = lax.rsqrt(spread + 1e-06)
        normed[:, :half] = (lo * inverse * gain[:, :half]).astype(BF)
        normed[:, half:] = (hi * inverse * gain[:, half:]).astype(BF)

    hidden = jax.nn.gelu(dot(normed[...], w_in[...]), approximate=True).astype(BF)
    total = hid_in[...] + dot(members, hidden)
    if not last:
        hid_out[...] = total
        return
    coarse = total.astype(BF)
    fine = (total - coarse.astype(F32)).astype(BF)
    terms = dot(jnp.concatenate([coarse, fine], axis=0), w_out[...])
    terms = terms[:CAP_DEV] + terms[CAP_DEV:]

    @pl.when(step == 0)
    def _():
        acc[...] = terms

    @pl.when(step > 0)
    def _():
        acc[...] += terms

    @pl.when(step == pl.num_programs(0) - 1)
    def _():
        out[...] = acc[...]


def mlp_chunk(i, last, low, slots, tokens, other, gain, fc_in, fc_out, hidden, states):
    rows, half = other.shape
    d, ff = fc_in.shape
    e = fc_out.shape[1]
    tile_in = pl.BlockSpec((CAP_DEV, FF_TILE), lambda j: (0, j))
    whole = pl.BlockSpec((CAP_DEV, d), lambda j: (0, 0))
    in_specs = [
        pl.BlockSpec(memory_space=pltpu.SMEM),
        pl.BlockSpec((1, rows), lambda j: (0, i)),
        pl.BlockSpec((rows, half), lambda j: (i, 0)),
        pl.BlockSpec((rows, half), lambda j: (0, 0)),
        pl.BlockSpec((1, d), lambda j: (0, 0)),
        pl.BlockSpec((d, FF_TILE), lambda j: (0, j)),
    ]
    args = [low, slots, tokens, other, gain, fc_in]
    scratch = [pltpu.VMEM((rows, d), BF)]
    if last:
        in_specs.append(pl.BlockSpec((FF_TILE, e), lambda j: (j, 0)))
        args.append(fc_out)
        first_shape = jax.ShapeDtypeStruct((CAP_DEV, e), F32)
        first_spec = pl.BlockSpec((CAP_DEV, e), lambda j: (0, 0))
        scratch.append(pltpu.VMEM((CAP_DEV, e), F32))
    else:
        first_shape = jax.ShapeDtypeStruct((CAP_DEV, ff), F32)
        first_spec = tile_in
    return pl.pallas_call(
        functools.partial(mlp_kernel, last),
        grid=(ff // FF_TILE,),
        in_specs=in_specs + [tile_in, whole],
        out_specs=[first_spec, whole],
        out_shape=[first_shape, jax.ShapeDtypeStruct((CAP_DEV, d), F32)],
        scratch_shapes=scratch,
        compiler_params=pltpu.CompilerParams(vmem_limit_bytes=52 << 20),
        cost_estimate=SMALL,
    )(*args, hidden, states)


def loss_kernel(last, scal, columns, texts, img, *refs):
    if last:
        gt_in, gi_out, gt_out, acc = refs
    else:
        gi_out, acc = refs
    step = pl.program_id(0)
    e = texts.shape[1]
    scale, bias = scal[0], scal[1]
    rows = img[:, :e]
    code = img[:, e:].astype(F32)
    marks = (code[:, 0:1] * 64.0 + code[:, 1:2]).astype(jnp.int32)
    logit = lax.dot_general(
        rows, texts[...], (((1,), (1,)), ((), ())), preferred_element_type=F32
    )
    logit = scale * logit + bias
    sign = jnp.where(marks == columns[...], 1.0, -1.0).astype(F32)
    weight = (-scale * sign * jax.nn.sigmoid(-sign * logit)).astype(BF)
    gi_out[...] = dot(weight, texts[...]).astype(gi_out.dtype)
    part = lax.dot_general(weight, rows, (((0,), (0,)), ((), ())), preferred_element_type=F32)

    @pl.when(step == 0)
    def _():
        acc[...] = gt_in[...] + part if last else part

    @pl.when(step > 0)
    def _():
        acc[...] += part

    if last:
        half = e // 2

        @pl.when(step == pl.num_programs(0) - 1)
        def _():
            for g in range(texts.shape[0] // CAP_DEV):
                for h in range(2):
                    gt_out[2 * g + h] = acc[
                        g * CAP_DEV : (g + 1) * CAP_DEV, h * half : (h + 1) * half
                    ].astype(BF)


def loss(last, scal, columns, texts, img, *gt_in):
    n, e = texts.shape
    total = img.shape[0]
    fixed = lambda shape: pl.BlockSpec(shape, lambda j: (0,) * len(shape))
    in_specs = [
        pl.BlockSpec(memory_space=pltpu.SMEM),
        fixed((1, n)),
        fixed((n, e)),
        pl.BlockSpec((IMG_TILE, img.shape[1]), lambda j: (j, 0)),
    ]
    gi_spec = pl.BlockSpec((IMG_TILE, e), lambda j: (j, 0))
    if last:
        in_specs.append(fixed((n, e)))
        shape = (2 * n // CAP_DEV, CAP_DEV, e // 2)
        out_specs = [gi_spec, fixed(shape)]
        out_shape = [
            jax.ShapeDtypeStruct((total, e), F32),
            jax.ShapeDtypeStruct(shape, BF),
        ]
        scratch = [pltpu.VMEM((n, e), F32)]
    else:
        out_specs = [gi_spec, fixed((n, e))]
        out_shape = [
            jax.ShapeDtypeStruct((total, e), BF),
            jax.ShapeDtypeStruct((n, e), F32),
        ]
        scratch = []
    return pl.pallas_call(
        functools.partial(loss_kernel, last),
        grid=(total // IMG_TILE,),
        in_specs=in_specs,
        out_specs=out_specs,
        out_shape=out_shape,
        scratch_shapes=scratch,
        compiler_params=pltpu.CompilerParams(vmem_limit_bytes=52 << 20),
        cost_estimate=SMALL,
    )(scal, columns, texts, img, *gt_in)


def on_device(
    tokens, norm_gain, fc_in, fc_out, projection, slots, images, labels, logit_scale, logit_bias
):
    zh, xl, core, xh = (lax.axis_index(a) for a in ("zh", "xl", "core", "xh"))
    low = xh == 0

    rows = tokens.shape[0] // CHUNKS
    others = [
        lax.ppermute(tokens[i * rows : (i + 1) * rows], MP, SWAP) for i in range(CHUNKS)
    ]

    imgs = images.astype(F32)
    img = (imgs * lax.rsqrt(jnp.sum(imgs * imgs, axis=1, keepdims=True) + 1e-06)).astype(BF)
    code = jnp.stack([labels // 64, labels % 64], axis=1).astype(F32).astype(BF)
    img = jnp.concatenate([img, jnp.pad(code, ((0, 0), (0, PAD - 2)))], axis=1)
    img_mine = jnp.concatenate(
        [img] + [lax.ppermute(img, "zh", shift(4, k)) for k in (1, 2, 3)], axis=0
    )

    members = slots[0][None, :] == jnp.arange(CAP_DEV, dtype=jnp.int32)[:, None]
    counts = jnp.sum(members.astype(F32), axis=1)
    hidden = jnp.zeros((CAP_DEV, fc_in.shape[1]), F32)
    states = jnp.zeros((CAP_DEV, fc_in.shape[0]), F32)
    flag = low.astype(jnp.int32).reshape(1)
    for i, other in enumerate(others):
        last = i == CHUNKS - 1
        if last:
            other, _ = lax.optimization_barrier((other, img_mine))
        hidden, states = mlp_chunk(
            i, last, flag, slots, tokens, other, norm_gain[None, :], fc_in, fc_out, hidden, states
        )
    partial_out, img_sent = lax.optimization_barrier((hidden, img_mine))
    img_other = lax.ppermute(img_sent, "core", SWAP)
    summed = partial_out + lax.ppermute(partial_out, MP, SWAP)
    pooled = ((states + summed) / counts[:, None]).astype(BF)

    emb = dot(pooled, projection)
    emb, img_other = lax.optimization_barrier((emb, img_other))
    before, across, after = [
        lax.ppermute(emb, ("xl", "xh"), ring_x(k)) for k in (1, 2, 3)
    ]
    near_low = xl == xh
    other_low = jnp.where(near_low, after, before)
    other_high = jnp.where(near_low, before, after)
    mine_low = jnp.where(low, emb, across)
    mine_high = jnp.where(low, across, emb)

    def normalised(lo, hi):
        squares = jnp.sum(lo * lo, axis=1, keepdims=True) + jnp.sum(hi * hi, axis=1, keepdims=True)
        inverse = lax.rsqrt(squares + 1e-06)
        return (lo * inverse).astype(BF), (hi * inverse).astype(BF)

    mine_low, mine_high = normalised(mine_low, mine_high)
    other_low, other_high = normalised(other_low, other_high)
    text_part = jnp.where(low, mine_low, mine_high)
    mine = jnp.concatenate([mine_low, mine_high], axis=1)
    other = jnp.concatenate([other_low, other_high], axis=1)
    first = xl == 0
    pair = jnp.concatenate([jnp.where(first, mine, other), jnp.where(first, other, mine)], axis=0)

    texts = lax.all_to_all(
        jnp.broadcast_to(pair[None], (8,) + pair.shape), ("zl", "y"), split_axis=0, concat_axis=0,
        tiled=True,
    ).reshape(16 * CAP_DEV, -1)
    zl_i, y_i, xl_i, cap_i = (
        lax.broadcasted_iota(jnp.int32, (2, 4, 2, CAP_DEV), d) for d in range(4)
    )
    columns = (((((zh * 2 + zl_i) * 2 + xl_i) * 4 + y_i) * 2 + core) * CAP_DEV + cap_i).reshape(1, -1)

    scal = jnp.concatenate([logit_scale, logit_bias])
    gi_send, gt = loss(False, scal, columns, texts, img_other)
    gi_got = lax.ppermute(gi_send, "core", SWAP)
    gi, gt = loss(True, scal, columns, texts, img_mine, gt)

    gi = gi + gi_got.astype(F32)
    grad_image = gi[:IMG_ROWS]
    for k in (1, 2, 3):
        back = gi[k * IMG_ROWS : (k + 1) * IMG_ROWS].astype(BF)
        grad_image += lax.ppermute(back, "zh", shift(4, -k)).astype(F32)

    got = lax.all_to_all(gt, ("zl", "y", "xl", "xh"), split_axis=0, concat_axis=0, tiled=True)
    grad_text = jnp.sum(got.astype(F32), axis=0)
    return (text_part, grad_image, grad_text)


def solution(mesh):
    fine = Mesh(mesh.devices.reshape(SIZES), AXES)
    every = DP + (MP,)
    placed = (
        P(DP, MP),
        P(),
        P(None, MP),
        P(MP, None),
        P(None, MP),
        P(DP, None),
        P(every, None),
        P(every),
        P(),
        P(),
    )
    return jax.shard_map(
        on_device,
        mesh=fine,
        in_specs=placed,
        out_specs=(P(DP, MP), P(every, None), P(DP, MP)),
        check_vma=False,
    )
```

```python
import functools
import jax
import jax.numpy as jnp
from jax import lax
from jax.experimental import pallas as pl
from jax.experimental.pallas import tpu as pltpu
from jax.sharding import Mesh, PartitionSpec as P

CAP_DEV = 32
ROW_TILE = 512
FF_TILE = 1024
IMG_ROWS = 128
GELU_A = 0.7978845608028654
GELU_B = GELU_A * 0.044715
PAD = 128
AXES = ("zh", "zl", "xl", "y", "core", "xh")
SIZES = (4, 2, 2, 4, 2, 2)
DP = ("zh", "zl", "xl", "y", "core")
MP = "xh"
BF = jnp.bfloat16
F32 = jnp.float32
SWAP = [(0, 1), (1, 0)]
LARGE = pl.CostEstimate(flops=10**10, bytes_accessed=1000, transcendentals=0)
SMALL = pl.CostEstimate(flops=1000, bytes_accessed=1000, transcendentals=0)


def dot(a, b):
    return jnp.dot(a, b, preferred_element_type=F32)


def shift(n, k):
    return [(i, (i + k) % n) for i in range(n)]


def mlp_kernel(row_tile, ff_tile, low, slot, own, other, gain, fc_in, fc_out, out, st_out, w_in, w_out, sems):
    rows, half = own.shape
    ff = w_in.shape[1]
    tiles = [pl.ds(j * ff_tile, ff_tile) for j in range(ff // ff_tile)]
    loads = [
        pltpu.make_async_copy(fc_in.at[:, t], w_in.at[:, t], sems.at[j])
        for j, t in enumerate(tiles)
    ]
    loads.append(pltpu.make_async_copy(fc_out, w_out, sems.at[len(tiles)]))
    for load in loads:
        load.start()
    size = 1.0 / (2 * half)
    is_low = low[0] == 1
    pooled = [jnp.zeros((CAP_DEV, ff_tile), F32) for _ in range(ff // ff_tile)]
    states = [jnp.zeros((CAP_DEV, half), F32) for _ in range(2)]
    for r in range(0, rows, row_tile):
        block = slice(r, r + row_tile)
        captions = lax.broadcasted_iota(jnp.int32, (CAP_DEV, row_tile), 0)
        members = (captions == slot[:, block]).astype(F32).astype(BF)
        mine = own[block, :]
        theirs = other[block, :]
        lo = jnp.where(is_low, mine, theirs)
        hi = jnp.where(is_low, theirs, mine)
        states[0] += dot(members, lo)
        states[1] += dot(members, hi)
        lo = lo.astype(F32)
        hi = hi.astype(F32)
        mean = (jnp.sum(lo, axis=1, keepdims=True) + jnp.sum(hi, axis=1, keepdims=True)) * size
        lo = lo - mean
        hi = hi - mean
        spread = (
            jnp.sum(lo * lo, axis=1, keepdims=True) + jnp.sum(hi * hi, axis=1, keepdims=True)
        ) * size
        inverse = lax.rsqrt(spread + 1e-06)
        normed = jnp.concatenate(
            [
                (lo * inverse * gain[:, :half]).astype(BF),
                (hi * inverse * gain[:, half:]).astype(BF),
            ],
            axis=1,
        )
        for j in range(ff // ff_tile):
            if r == 0:
                loads[j].wait()
            pre = dot(normed, w_in[:, j * ff_tile : (j + 1) * ff_tile])
            pre_half = 0.5 * pre
            bend = jnp.tanh(pre * (GELU_A + GELU_B * (pre * pre)))
            hidden = (pre_half + pre_half * bend).astype(BF)
            pooled[j] += dot(members, hidden)
    st_out[:, :half] = states[0]
    st_out[:, half:] = states[1]
    loads[-1].wait()
    terms = jnp.zeros((2 * CAP_DEV, w_out.shape[1]), F32)
    for j in range(ff // ff_tile):
        coarse = pooled[j].astype(BF)
        fine = (pooled[j] - coarse.astype(F32)).astype(BF)
        terms += dot(
            jnp.concatenate([coarse, fine], axis=0), w_out[j * ff_tile : (j + 1) * ff_tile, :]
        )
    out[...] = terms[:CAP_DEV] + terms[CAP_DEV:]


def weights_of(scal, columns, texts, img):
    e = texts.shape[1]
    scale, bias = scal[0], scal[1]
    code = img[:, e:].astype(F32)
    marks = (code[:, 0:1] * 64.0 + code[:, 1:2]).astype(jnp.int32)
    logit = lax.dot_general(
        img[:, :e], texts, (((1,), (1,)), ((), ())), preferred_element_type=F32
    )
    logit = scale * logit + bias
    sign = jnp.where(marks == columns[...], 1.0, -1.0).astype(F32)
    return (-scale * sign * jax.nn.sigmoid(-sign * logit)).astype(BF)


def first_kernel(scal, columns, emb, img, texts, weight, gi):
    half = emb.shape[3]
    for g in range(emb.shape[0]):
        lo = emb[g, 0].astype(F32)
        hi = emb[g, 1].astype(F32)
        squares = jnp.sum(lo * lo, axis=1, keepdims=True) + jnp.sum(hi * hi, axis=1, keepdims=True)
        inverse = lax.rsqrt(squares + 1e-06)
        rows = slice(g * CAP_DEV, (g + 1) * CAP_DEV)
        texts[rows, :half] = (lo * inverse).astype(BF)
        texts[rows, half:] = (hi * inverse).astype(BF)
    w = weights_of(scal, columns, texts[...], img)
    weight[...] = w
    gi[...] = dot(w, texts[...]).astype(BF)


def second_kernel(scal, columns, texts, img, weight):
    weight[...] = weights_of(scal, columns, texts[...], img)


def image_kernel(place, weight, texts, got, own, first, second, third, total):
    total[...] = dot(weight[...], texts[...]) + got[...].astype(F32)
    rows = own.shape[0]
    for k, out in enumerate((own, first, second, third)):
        slot = lax.rem(place[0] + (4 - k), 4)
        out[...] = total[pl.ds(pl.multiple_of(slot * rows, rows), rows), :].astype(out.dtype)


def text_kernel(weight_a, img_a, weight_b, img_b, out):
    half = out.shape[3]
    e = 2 * half
    turned = (((0,), (0,)), ((), ()))
    gt = lax.dot_general(weight_a[...], img_a[:, :e], turned, preferred_element_type=F32)
    gt += lax.dot_general(weight_b[...], img_b[:, :e], turned, preferred_element_type=F32)
    groups = out.shape[0] // 2
    for z in range(2):
        for g in range(groups):
            row = (z * groups + g) * CAP_DEV
            for h in range(2):
                out[2 * g + h, z] = gt[row : row + CAP_DEV, h * half : (h + 1) * half].astype(BF)


def call(kernel, args, outs, scalars=0, far=(), scratch=(), cost=SMALL):
    in_specs = [
        pl.BlockSpec(
            memory_space=pltpu.SMEM if i < scalars else pltpu.HBM if i in far else pltpu.VMEM
        )
        for i in range(len(args))
    ]
    return pl.pallas_call(
        kernel,
        in_specs=in_specs,
        out_specs=[pl.BlockSpec(memory_space=pltpu.VMEM) for _ in outs],
        out_shape=[jax.ShapeDtypeStruct(shape, dtype) for shape, dtype in outs],
        scratch_shapes=list(scratch),
        compiler_params=pltpu.CompilerParams(vmem_limit_bytes=54 << 20),
        cost_estimate=cost,
    )(*args)


def on_device(
    tokens, norm_gain, fc_in, fc_out, projection, slots, images, labels, logit_scale, logit_bias
):
    zh, core, xh = (lax.axis_index(a) for a in ("zh", "core", "xh"))
    low = xh == 0

    other = lax.ppermute(tokens, MP, SWAP)

    imgs = images.astype(F32)
    img = (imgs * lax.rsqrt(jnp.sum(imgs * imgs, axis=1, keepdims=True) + 1e-06)).astype(BF)
    code = jnp.stack([labels // 64, labels % 64], axis=1).astype(F32).astype(BF)
    img = jnp.concatenate([img, jnp.pad(code, ((0, 0), (0, PAD - 2)))], axis=1)
    img_mine = lax.all_to_all(
        jnp.broadcast_to(img[None], (4,) + img.shape), "zh", split_axis=0, concat_axis=0, tiled=True
    ).reshape(4 * IMG_ROWS, -1)

    members = slots[0][None, :] == jnp.arange(CAP_DEV, dtype=jnp.int32)[:, None]
    counts = jnp.sum(members.astype(F32), axis=1)
    flag = low.astype(jnp.int32).reshape(1)
    partial_out, states = call(
        functools.partial(mlp_kernel, ROW_TILE, FF_TILE),
        (flag, slots, tokens, other, norm_gain[None, :], fc_in, fc_out),
        [((CAP_DEV, fc_out.shape[1]), F32), ((CAP_DEV, fc_in.shape[0]), F32)],
        1,
        (5, 6),
        (
            pltpu.VMEM(fc_in.shape, BF),
            pltpu.VMEM(fc_out.shape, BF),
            pltpu.SemaphoreType.DMA((fc_in.shape[1] // FF_TILE + 1,)),
        ),
        LARGE,
    )
    summed = partial_out + lax.ppermute(partial_out, MP, SWAP)
    pooled = ((states + summed) / counts[:, None]).astype(BF)
    emb = dot(pooled, projection)

    group = ("zl", "y", "xl", "xh")
    sent = jnp.broadcast_to(emb.astype(BF)[None], (32,) + emb.shape)
    embs = lax.all_to_all(sent, group, split_axis=0, concat_axis=0, tiled=True)
    embs = embs.reshape((16, 2) + emb.shape)
    img_sent, _ = lax.optimization_barrier((img_mine, emb))
    img_other = lax.ppermute(img_sent, "core", SWAP)

    zl_i, y_i, xl_i, cap_i = (
        lax.broadcasted_iota(jnp.int32, (2, 4, 2, CAP_DEV), d) for d in range(4)
    )
    columns = (((((zh * 2 + zl_i) * 2 + xl_i) * 4 + y_i) * 2 + core) * CAP_DEV + cap_i).reshape(1, -1)
    scal = jnp.concatenate([logit_scale, logit_bias])
    n, e = 16 * CAP_DEV, fc_in.shape[0]
    images_half = img_mine.shape[0]
    texts, weight_other, gi_send = call(
        first_kernel,
        (scal, columns, embs, img_other),
        [((n, e), BF), ((images_half, n), BF), ((images_half, e), BF)],
        1,
    )
    gi_got = lax.ppermute(gi_send, "core", SWAP)
    (weight_mine,) = call(
        second_kernel, (scal, columns, texts, img_mine), [((images_half, n), BF)], 1
    )

    gi_got, weight_mine = lax.optimization_barrier((gi_got, weight_mine))
    grad_image, *rest = call(
        image_kernel,
        (zh.astype(jnp.int32).reshape(1), weight_mine, texts, gi_got),
        [((IMG_ROWS, e), F32)] + [((IMG_ROWS, e), BF)] * 3,
        1,
        scratch=(pltpu.VMEM((images_half, e), F32),),
    )
    for k, part in enumerate(rest):
        grad_image += lax.ppermute(part, "zh", shift(4, -k - 1)).astype(F32)

    weight_mine, _ = lax.optimization_barrier((weight_mine, rest[0]))
    (gt,) = call(
        text_kernel,
        (weight_other, img_other, weight_mine, img_mine),
        [((16, 2, CAP_DEV, e // 2), BF)],
    )
    got = lax.all_to_all(gt, ("y", "xl", "xh"), split_axis=0, concat_axis=0, tiled=True)
    gathered = jnp.sum(got.astype(F32), axis=0)
    front = lax.axis_index("zl") == 0
    keep = jnp.where(front, gathered[0], gathered[1])
    give = jnp.where(front, gathered[1], gathered[0])
    grad_text = keep + lax.ppermute(give, "zl", SWAP)

    own_emb = lax.dynamic_index_in_dim(
        embs, (lax.axis_index("zl") * 4 + lax.axis_index("y")) * 2 + lax.axis_index("xl"), 0, False
    ).astype(F32)
    squares = jnp.sum(own_emb * own_emb, axis=(0, 2))
    text_part = (emb * lax.rsqrt(squares + 1e-06)[:, None]).astype(BF)
    return (text_part, grad_image, grad_text)


def solution(mesh):
    fine = Mesh(mesh.devices.reshape(SIZES), AXES)
    every = DP + (MP,)
    placed = (
        P(DP, MP),
        P(),
        P(None, MP),
        P(MP, None),
        P(None, MP),
        P(DP, None),
        P(every, None),
        P(every),
        P(),
        P(),
    )
    return jax.shard_map(
        on_device,
        mesh=fine,
        in_specs=placed,
        out_specs=(P(DP, MP), P(every, None), P(DP, MP)),
        check_vma=False,
    )
```

```python
import functools
import jax
import jax.numpy as jnp
from jax import lax
from jax.experimental import pallas as pl
from jax.experimental.pallas import tpu as pltpu
from jax.sharding import Mesh, PartitionSpec as P

CAP_DEV = 32
ROW_TILE = 512
FF_TILE = 1024
IMG_ROWS = 128
GELU_A = 0.7978845608028654
GELU_B = GELU_A * 0.044715
PAD = 128
AXES = ("zh", "zl", "xl", "y", "core", "xh")
SIZES = (4, 2, 2, 4, 2, 2)
DP = ("zh", "zl", "xl", "y", "core")
MP = "xh"
BF = jnp.bfloat16
F32 = jnp.float32
SWAP = [(0, 1), (1, 0)]
LARGE = pl.CostEstimate(flops=10**10, bytes_accessed=1000, transcendentals=0)
SMALL = pl.CostEstimate(flops=1000, bytes_accessed=1000, transcendentals=0)


def dot(a, b):
    return jnp.dot(a, b, preferred_element_type=F32)


def shift(n, k):
    return [(i, (i + k) % n) for i in range(n)]


def head_kernel(mine, got, states, counts, projection, emb, sent, block, sems):
    pooled = ((states[...] + (mine[...] + got[...])) / counts[...]).astype(BF)
    result = dot(pooled, projection[...])
    block[...] = jnp.broadcast_to(result.astype(BF)[None], block.shape)
    n = block.shape[0]
    stores = [
        pltpu.make_async_copy(block, sent.at[pl.ds(i * n, n)], sems.at[i])
        for i in range(sent.shape[0] // n)
    ]
    for store in stores:
        store.start()
    emb[...] = result
    for store in stores:
        store.wait()


def mlp_kernel(
    row_tile, ff_tile, low, slot, tokens, arrived, gain, fc_in, fc_out, out, st_out,
    own, other, w_in, w_out, sems
):
    rows, half = own.shape
    ff = w_in.shape[1]
    blocks = [slice(r, r + row_tile) for r in range(0, rows, row_tile)]
    tiles = [slice(j, j + ff_tile) for j in range(0, ff, ff_tile)]
    pairs = []
    for block in blocks:
        pairs.append([(tokens.at[block, :], own.at[block, :])])
        pairs[-1].append((arrived.at[block, :], other.at[block, :]))
    for j, tile in enumerate(tiles):
        pairs.insert(2 * j + 1, [(fc_in.at[:, tile], w_in.at[:, tile])])
    pairs.append([(fc_out, w_out)])
    loads = [
        [pltpu.make_async_copy(a, b, sems.at[i, k]) for k, (a, b) in enumerate(pair)]
        for i, pair in enumerate(pairs)
    ]
    for group in loads:
        for load in group:
            load.start()
    size = 1.0 / (2 * half)
    is_low = low[0] == 1
    pooled = [jnp.zeros((CAP_DEV, ff_tile), F32) for _ in range(ff // ff_tile)]
    states = [jnp.zeros((CAP_DEV, half), F32) for _ in range(2)]
    for i, block in enumerate(blocks):
        for load in loads[2 * i]:
            load.wait()
        captions = lax.broadcasted_iota(jnp.int32, (CAP_DEV, row_tile), 0)
        members = (captions == slot[:, block]).astype(F32).astype(BF)
        mine = own[block, :]
        theirs = other[block, :]
        lo = jnp.where(is_low, mine, theirs)
        hi = jnp.where(is_low, theirs, mine)
        states[0] += dot(members, lo)
        states[1] += dot(members, hi)
        lo = lo.astype(F32)
        hi = hi.astype(F32)
        mean = (jnp.sum(lo, axis=1, keepdims=True) + jnp.sum(hi, axis=1, keepdims=True)) * size
        lo = lo - mean
        hi = hi - mean
        spread = (
            jnp.sum(lo * lo, axis=1, keepdims=True) + jnp.sum(hi * hi, axis=1, keepdims=True)
        ) * size
        inverse = lax.rsqrt(spread + 1e-06)
        normed = jnp.concatenate(
            [
                (lo * inverse * gain[:, :half]).astype(BF),
                (hi * inverse * gain[:, half:]).astype(BF),
            ],
            axis=1,
        )
        for j in range(ff // ff_tile):
            if i == 0:
                loads[2 * j + 1][0].wait()
            pre = dot(normed, w_in[:, j * ff_tile : (j + 1) * ff_tile])
            pre_half = 0.5 * pre
            bend = jnp.tanh(pre * (GELU_A + GELU_B * (pre * pre)))
            hidden = (pre_half + pre_half * bend).astype(BF)
            pooled[j] += dot(members, hidden)
    st_out[:, :half] = states[0]
    st_out[:, half:] = states[1]
    loads[-1][0].wait()
    terms = jnp.zeros((2 * CAP_DEV, w_out.shape[1]), F32)
    for j in range(ff // ff_tile):
        coarse = pooled[j].astype(BF)
        fine = (pooled[j] - coarse.astype(F32)).astype(BF)
        terms += dot(
            jnp.concatenate([coarse, fine], axis=0), w_out[j * ff_tile : (j + 1) * ff_tile, :]
        )
    out[...] = terms[:CAP_DEV] + terms[CAP_DEV:]


def weights_of(scal, columns, texts, img):
    e = texts.shape[1]
    scale, bias = scal[0], scal[1]
    code = img[:, e:].astype(F32)
    marks = (code[:, 0:1] * 64.0 + code[:, 1:2]).astype(jnp.int32)
    logit = lax.dot_general(
        img[:, :e], texts, (((1,), (1,)), ((), ())), preferred_element_type=F32
    )
    logit = scale * logit + bias
    sign = jnp.where(marks == columns[...], 1.0, -1.0).astype(F32)
    return (-scale * sign * jax.nn.sigmoid(-sign * logit)).astype(BF)


def first_kernel(scal, place, columns, emb, exact, img, own_text, texts, weight, gi):
    half = emb.shape[3]
    for g in range(emb.shape[0]):
        lo = emb[g, 0].astype(F32)
        hi = emb[g, 1].astype(F32)
        squares = jnp.sum(lo * lo, axis=1, keepdims=True) + jnp.sum(hi * hi, axis=1, keepdims=True)
        inverse = lax.rsqrt(squares + 1e-06)
        rows = slice(g * CAP_DEV, (g + 1) * CAP_DEV)
        texts[rows, :half] = (lo * inverse).astype(BF)
        texts[rows, half:] = (hi * inverse).astype(BF)
    lo = emb[place[0], 0].astype(F32)
    hi = emb[place[0], 1].astype(F32)
    squares = jnp.sum(lo * lo, axis=1, keepdims=True) + jnp.sum(hi * hi, axis=1, keepdims=True)
    own_text[...] = (exact[...] * lax.rsqrt(squares + 1e-06)).astype(BF)
    w = weights_of(scal, columns, texts[...], img)
    weight[...] = w
    gi[...] = dot(w, texts[...]).astype(BF)


def second_kernel(scal, columns, texts, img, weight):
    weight[...] = weights_of(scal, columns, texts[...], img)


def image_kernel(place, weight, texts, got, own, first, second, third, total):
    total[...] = dot(weight[...], texts[...]) + got[...].astype(F32)
    rows = own.shape[0]
    for k, out in enumerate((own, first, second, third)):
        slot = lax.rem(place[0] + (4 - k), 4)
        out[...] = total[pl.ds(pl.multiple_of(slot * rows, rows), rows), :].astype(out.dtype)


def text_kernel(weight_a, img_a, weight_b, img_b, out):
    half = out.shape[3]
    e = 2 * half
    turned = (((0,), (0,)), ((), ()))
    gt = lax.dot_general(weight_a[...], img_a[:, :e], turned, preferred_element_type=F32)
    gt += lax.dot_general(weight_b[...], img_b[:, :e], turned, preferred_element_type=F32)
    groups = out.shape[0] // 2
    for z in range(2):
        for g in range(groups):
            row = (z * groups + g) * CAP_DEV
            for h in range(2):
                out[2 * g + h, z] = gt[row : row + CAP_DEV, h * half : (h + 1) * half].astype(BF)


def call(kernel, args, outs, scalars=0, far=(), free=(), far_out=(), scratch=(), cost=SMALL, limit=20):
    in_specs = [
        pl.BlockSpec(
            memory_space=pltpu.SMEM
            if i < scalars
            else pltpu.HBM if i in far else pl.ANY if i in free else pltpu.VMEM
        )
        for i in range(len(args))
    ]
    return pl.pallas_call(
        kernel,
        in_specs=in_specs,
        out_specs=[
            pl.BlockSpec(memory_space=pltpu.HBM if i in far_out else pltpu.VMEM)
            for i in range(len(outs))
        ],
        out_shape=[jax.ShapeDtypeStruct(shape, dtype) for shape, dtype in outs],
        scratch_shapes=list(scratch),
        compiler_params=pltpu.CompilerParams(vmem_limit_bytes=limit << 20),
        cost_estimate=cost,
    )(*args)


def on_device(
    tokens, norm_gain, fc_in, fc_out, projection, slots, images, labels, logit_scale, logit_bias
):
    zh, core, xh = (lax.axis_index(a) for a in ("zh", "core", "xh"))
    low = xh == 0

    other = lax.ppermute(tokens, MP, SWAP)

    imgs = images.astype(F32)
    img = (imgs * lax.rsqrt(jnp.sum(imgs * imgs, axis=1, keepdims=True) + 1e-06)).astype(BF)
    code = jnp.stack([labels // 64, labels % 64], axis=1).astype(F32).astype(BF)
    img = jnp.concatenate([img, jnp.pad(code, ((0, 0), (0, PAD - 2)))], axis=1)
    img_mine = lax.all_to_all(
        jnp.broadcast_to(img[None], (4,) + img.shape), "zh", split_axis=0, concat_axis=0, tiled=True
    ).reshape(4 * IMG_ROWS, -1)

    members = slots[0][None, :] == jnp.arange(CAP_DEV, dtype=jnp.int32)[:, None]
    counts = jnp.sum(members.astype(F32), axis=1)
    flag = low.astype(jnp.int32).reshape(1)
    partial_out, states = call(
        functools.partial(mlp_kernel, ROW_TILE, FF_TILE),
        (flag, slots, tokens, other, norm_gain[None, :], fc_in, fc_out),
        [((CAP_DEV, fc_out.shape[1]), F32), ((CAP_DEV, fc_in.shape[0]), F32)],
        1,
        far=(2, 5, 6),
        free=(3,),
        scratch=(
            pltpu.VMEM(tokens.shape, BF),
            pltpu.VMEM(tokens.shape, BF),
            pltpu.VMEM(fc_in.shape, BF),
            pltpu.VMEM(fc_out.shape, BF),
            pltpu.SemaphoreType.DMA((5, 2)),
        ),
        cost=LARGE,
        limit=48,
    )
    emb, sent = call(
        head_kernel,
        (partial_out, lax.ppermute(partial_out, MP, SWAP), states, counts[:, None], projection),
        [((CAP_DEV, projection.shape[1]), F32), ((32, CAP_DEV, projection.shape[1]), BF)],
        far_out=(1,),
        limit=60,
        scratch=(
            pltpu.VMEM((8, CAP_DEV, projection.shape[1]), BF),
            pltpu.SemaphoreType.DMA((4,)),
        ),
    )

    group = ("zl", "y", "xl", "xh")
    embs = lax.all_to_all(sent, group, split_axis=0, concat_axis=0, tiled=True)
    embs = embs.reshape((16, 2) + emb.shape)
    img_sent, _ = lax.optimization_barrier((img_mine, emb))
    img_other = lax.ppermute(img_sent, "core", SWAP)

    zl_i, y_i, xl_i, cap_i = (
        lax.broadcasted_iota(jnp.int32, (2, 4, 2, CAP_DEV), d) for d in range(4)
    )
    columns = (((((zh * 2 + zl_i) * 2 + xl_i) * 4 + y_i) * 2 + core) * CAP_DEV + cap_i).reshape(1, -1)
    scal = jnp.concatenate([logit_scale, logit_bias])
    n, e = 16 * CAP_DEV, fc_in.shape[0]
    images_half = img_mine.shape[0]
    zl, y, xl = (lax.axis_index(a) for a in ("zl", "y", "xl"))
    place = ((zl * 4 + y) * 2 + xl).astype(jnp.int32).reshape(1)
    text_part, texts, weight_other, gi_send = call(
        first_kernel,
        (scal, place, columns, embs, emb, img_other),
        [(emb.shape, BF), ((n, e), BF), ((images_half, n), BF), ((images_half, e), BF)],
        2,
    )
    gi_got = lax.ppermute(gi_send, "core", SWAP)
    (weight_mine,) = call(
        second_kernel, (scal, columns, texts, img_mine), [((images_half, n), BF)], 1
    )

    gi_got, weight_mine = lax.optimization_barrier((gi_got, weight_mine))
    grad_image, *rest = call(
        image_kernel,
        (zh.astype(jnp.int32).reshape(1), weight_mine, texts, gi_got),
        [((IMG_ROWS, e), F32)] + [((IMG_ROWS, e), BF)] * 3,
        1,
        scratch=(pltpu.VMEM((images_half, e), F32),),
    )
    for k, part in enumerate(rest):
        grad_image += lax.ppermute(part, "zh", shift(4, -k - 1)).astype(F32)

    weight_mine, _ = lax.optimization_barrier((weight_mine, rest[0]))
    (gt,) = call(
        text_kernel,
        (weight_other, img_other, weight_mine, img_mine),
        [((16, 2, CAP_DEV, e // 2), BF)],
    )
    got = lax.all_to_all(gt, ("y", "xl", "xh"), split_axis=0, concat_axis=0, tiled=True)
    gathered = jnp.sum(got.astype(F32), axis=0)
    front = zl == 0
    keep = jnp.where(front, gathered[0], gathered[1])
    give = jnp.where(front, gathered[1], gathered[0])
    grad_text = keep + lax.ppermute(give, "zl", SWAP)

    return (text_part, grad_image, grad_text)


def solution(mesh):
    fine = Mesh(mesh.devices.reshape(SIZES), AXES)
    every = DP + (MP,)
    placed = (
        P(DP, MP),
        P(),
        P(None, MP),
        P(MP, None),
        P(None, MP),
        P(DP, None),
        P(every, None),
        P(every),
        P(),
        P(),
    )
    return jax.shard_map(
        on_device,
        mesh=fine,
        in_specs=placed,
        out_specs=(P(DP, MP), P(every, None), P(DP, MP)),
        check_vma=False,
    )
```

```python
import functools
import jax
import jax.numpy as jnp
from jax import lax
from jax.experimental import pallas as pl
from jax.experimental.pallas import tpu as pltpu
from jax.sharding import Mesh, PartitionSpec as P

CAP_DEV = 32
ROW_TILE = 512
FF_TILE = 1024
IMG_ROWS = 128
GELU_A = 0.7978845608028654
GELU_B = GELU_A * 0.044715
PAD = 128
IMAGE_LIMIT = 54
TEXT_LIMIT = 20
AXES = ("zh", "zl", "xl", "y", "core", "xh")
SIZES = (4, 2, 2, 4, 2, 2)
DP = ("zh", "zl", "xl", "y", "core")
MP = "xh"
BF = jnp.bfloat16
F32 = jnp.float32
SWAP = [(0, 1), (1, 0)]
LARGE = pl.CostEstimate(flops=10**10, bytes_accessed=1000, transcendentals=0)
SMALL = pl.CostEstimate(flops=1000, bytes_accessed=1000, transcendentals=0)


def dot(a, b):
    return jnp.dot(a, b, preferred_element_type=F32)


def shift(n, k):
    return [(i, (i + k) % n) for i in range(n)]


def mlp_kernel(
    row_tile, ff_tile, low, slot, tokens, arrived, gain, fc_in, fc_out, out, st_out,
    own, other, w_in, w_out, sems
):
    rows, half = own.shape
    ff = w_in.shape[1]
    blocks = [slice(r, r + row_tile) for r in range(0, rows, row_tile)]
    tiles = [slice(j, j + ff_tile) for j in range(0, ff, ff_tile)]
    pairs = []
    for block in blocks:
        pairs.append([(tokens.at[block, :], own.at[block, :])])
        pairs[-1].append((arrived.at[block, :], other.at[block, :]))
    for j, tile in enumerate(tiles):
        pairs.insert(2 * j + 1, [(fc_in.at[:, tile], w_in.at[:, tile])])
    pairs.append([(fc_out, w_out)])
    loads = [
        [pltpu.make_async_copy(a, b, sems.at[i, k]) for k, (a, b) in enumerate(pair)]
        for i, pair in enumerate(pairs)
    ]
    for group in loads:
        for load in group:
            load.start()
    size = 1.0 / (2 * half)
    is_low = low[0] == 1
    pooled = [jnp.zeros((CAP_DEV, ff_tile), F32) for _ in range(ff // ff_tile)]
    states = [jnp.zeros((CAP_DEV, half), F32) for _ in range(2)]
    for i, block in enumerate(blocks):
        for load in loads[2 * i]:
            load.wait()
        captions = lax.broadcasted_iota(jnp.int32, (CAP_DEV, row_tile), 0)
        members = (captions == slot[:, block]).astype(F32).astype(BF)
        mine = own[block, :]
        theirs = other[block, :]
        lo = jnp.where(is_low, mine, theirs)
        hi = jnp.where(is_low, theirs, mine)
        states[0] += dot(members, lo)
        states[1] += dot(members, hi)
        lo = lo.astype(F32)
        hi = hi.astype(F32)
        mean = (jnp.sum(lo, axis=1, keepdims=True) + jnp.sum(hi, axis=1, keepdims=True)) * size
        lo = lo - mean
        hi = hi - mean
        spread = (
            jnp.sum(lo * lo, axis=1, keepdims=True) + jnp.sum(hi * hi, axis=1, keepdims=True)
        ) * size
        inverse = lax.rsqrt(spread + 1e-06)
        normed = jnp.concatenate(
            [
                (lo * inverse * gain[:, :half]).astype(BF),
                (hi * inverse * gain[:, half:]).astype(BF),
            ],
            axis=1,
        )
        for j in range(ff // ff_tile):
            if i == 0:
                loads[2 * j + 1][0].wait()
            pre = dot(normed, w_in[:, j * ff_tile : (j + 1) * ff_tile])
            pre_half = 0.5 * pre
            bend = jnp.tanh(pre * (GELU_A + GELU_B * (pre * pre)))
            hidden = (pre_half + pre_half * bend).astype(BF)
            pooled[j] += dot(members, hidden)
    st_out[:, :half] = states[0]
    st_out[:, half:] = states[1]
    loads[-1][0].wait()
    terms = jnp.zeros((2 * CAP_DEV, w_out.shape[1]), F32)
    for j in range(ff // ff_tile):
        coarse = pooled[j].astype(BF)
        fine = (pooled[j] - coarse.astype(F32)).astype(BF)
        terms += dot(
            jnp.concatenate([coarse, fine], axis=0), w_out[j * ff_tile : (j + 1) * ff_tile, :]
        )
    out[...] = terms[:CAP_DEV] + terms[CAP_DEV:]


def weights_of(scal, columns, texts, img):
    e = texts.shape[1]
    scale, bias = scal[0], scal[1]
    code = img[:, e:].astype(F32)
    marks = (code[:, 0:1] * 64.0 + code[:, 1:2]).astype(jnp.int32)
    logit = lax.dot_general(
        img[:, :e], texts, (((1,), (1,)), ((), ())), preferred_element_type=F32
    )
    logit = scale * logit + bias
    sign = jnp.where(marks == columns[...], 1.0, -1.0).astype(F32)
    return (-scale * sign * jax.nn.sigmoid(-sign * logit)).astype(BF)


def first_kernel(scal, place, columns, emb, exact, img, own_text, texts, weight, gi):
    half = emb.shape[3]
    for g in range(emb.shape[0]):
        lo = emb[g, 0].astype(F32)
        hi = emb[g, 1].astype(F32)
        squares = jnp.sum(lo * lo, axis=1, keepdims=True) + jnp.sum(hi * hi, axis=1, keepdims=True)
        inverse = lax.rsqrt(squares + 1e-06)
        rows = slice(g * CAP_DEV, (g + 1) * CAP_DEV)
        texts[rows, :half] = (lo * inverse).astype(BF)
        texts[rows, half:] = (hi * inverse).astype(BF)
    lo = emb[place[0], 0].astype(F32)
    hi = emb[place[0], 1].astype(F32)
    squares = jnp.sum(lo * lo, axis=1, keepdims=True) + jnp.sum(hi * hi, axis=1, keepdims=True)
    own_text[...] = (exact[...] * lax.rsqrt(squares + 1e-06)).astype(BF)
    w = weights_of(scal, columns, texts[...], img)
    weight[...] = w
    gi[...] = dot(w, texts[...]).astype(BF)


def second_kernel(scal, columns, texts, img, weight):
    weight[...] = weights_of(scal, columns, texts[...], img)


def image_kernel(place, weight, texts, got, own, first, second, third, total):
    total[...] = dot(weight[...], texts[...]) + got[...].astype(F32)
    rows = own.shape[0]
    for k, out in enumerate((own, first, second, third)):
        slot = lax.rem(place[0] + (4 - k), 4)
        out[...] = total[pl.ds(pl.multiple_of(slot * rows, rows), rows), :].astype(out.dtype)


def text_kernel(weight_a, img_a, weight_b, img_b, out):
    half = out.shape[3]
    e = 2 * half
    turned = (((0,), (0,)), ((), ()))
    gt = lax.dot_general(weight_a[...], img_a[:, :e], turned, preferred_element_type=F32)
    gt += lax.dot_general(weight_b[...], img_b[:, :e], turned, preferred_element_type=F32)
    groups = out.shape[0] // 2
    for z in range(2):
        for g in range(groups):
            row = (z * groups + g) * CAP_DEV
            for h in range(2):
                out[2 * g + h, z] = gt[row : row + CAP_DEV, h * half : (h + 1) * half].astype(BF)


def call(kernel, args, outs, scalars=0, far=(), free=(), scratch=(), cost=SMALL, limit=20):
    in_specs = [
        pl.BlockSpec(
            memory_space=pltpu.SMEM
            if i < scalars
            else pltpu.HBM if i in far else pl.ANY if i in free else pltpu.VMEM
        )
        for i in range(len(args))
    ]
    return pl.pallas_call(
        kernel,
        in_specs=in_specs,
        out_specs=[pl.BlockSpec(memory_space=pltpu.VMEM) for _ in outs],
        out_shape=[jax.ShapeDtypeStruct(shape, dtype) for shape, dtype in outs],
        scratch_shapes=list(scratch),
        compiler_params=pltpu.CompilerParams(vmem_limit_bytes=limit << 20),
        cost_estimate=cost,
    )(*args)


def on_device(
    tokens, norm_gain, fc_in, fc_out, projection, slots, images, labels, logit_scale, logit_bias
):
    zh, core, xh = (lax.axis_index(a) for a in ("zh", "core", "xh"))
    low = xh == 0

    other = lax.ppermute(tokens, MP, SWAP)

    imgs = images.astype(F32)
    img = (imgs * lax.rsqrt(jnp.sum(imgs * imgs, axis=1, keepdims=True) + 1e-06)).astype(BF)
    code = jnp.stack([labels // 64, labels % 64], axis=1).astype(F32).astype(BF)
    img = jnp.concatenate([img, jnp.pad(code, ((0, 0), (0, PAD - 2)))], axis=1)
    img_mine = lax.all_to_all(
        jnp.broadcast_to(img[None], (4,) + img.shape), "zh", split_axis=0, concat_axis=0, tiled=True
    ).reshape(4 * IMG_ROWS, -1)

    members = slots[0][None, :] == jnp.arange(CAP_DEV, dtype=jnp.int32)[:, None]
    counts = jnp.sum(members.astype(F32), axis=1)
    flag = low.astype(jnp.int32).reshape(1)
    partial_out, states = call(
        functools.partial(mlp_kernel, ROW_TILE, FF_TILE),
        (flag, slots, tokens, other, norm_gain[None, :], fc_in, fc_out),
        [((CAP_DEV, fc_out.shape[1]), F32), ((CAP_DEV, fc_in.shape[0]), F32)],
        1,
        far=(2, 5, 6),
        free=(3,),
        scratch=(
            pltpu.VMEM(tokens.shape, BF),
            pltpu.VMEM(tokens.shape, BF),
            pltpu.VMEM(fc_in.shape, BF),
            pltpu.VMEM(fc_out.shape, BF),
            pltpu.SemaphoreType.DMA((5, 2)),
        ),
        cost=LARGE,
        limit=48,
    )
    summed = partial_out + lax.ppermute(partial_out, MP, SWAP)
    pooled = ((states + summed) / counts[:, None]).astype(BF)
    emb = dot(pooled, projection)
    sent = jnp.broadcast_to(emb.astype(BF)[None], (32,) + emb.shape)

    group = ("zl", "y", "xl", "xh")
    embs = lax.all_to_all(sent, group, split_axis=0, concat_axis=0, tiled=True)
    embs = embs.reshape((16, 2) + emb.shape)
    img_sent, _ = lax.optimization_barrier((img_mine, emb))
    img_other = lax.ppermute(img_sent, "core", SWAP)

    zl_i, y_i, xl_i, cap_i = (
        lax.broadcasted_iota(jnp.int32, (2, 4, 2, CAP_DEV), d) for d in range(4)
    )
    columns = (((((zh * 2 + zl_i) * 2 + xl_i) * 4 + y_i) * 2 + core) * CAP_DEV + cap_i).reshape(1, -1)
    scal = jnp.concatenate([logit_scale, logit_bias])
    n, e = 16 * CAP_DEV, fc_in.shape[0]
    images_half = img_mine.shape[0]
    zl, y, xl = (lax.axis_index(a) for a in ("zl", "y", "xl"))
    place = ((zl * 4 + y) * 2 + xl).astype(jnp.int32).reshape(1)
    text_part, texts, weight_other, gi_send = call(
        first_kernel,
        (scal, place, columns, embs, emb, img_other),
        [(emb.shape, BF), ((n, e), BF), ((images_half, n), BF), ((images_half, e), BF)],
        2,
    )
    gi_got = lax.ppermute(gi_send, "core", SWAP)
    (weight_mine,) = call(
        second_kernel, (scal, columns, texts, img_mine), [((images_half, n), BF)], 1
    )

    gi_got, weight_mine = lax.optimization_barrier((gi_got, weight_mine))
    grad_image, *rest = call(
        image_kernel,
        (zh.astype(jnp.int32).reshape(1), weight_mine, texts, gi_got),
        [((IMG_ROWS, e), F32)] + [((IMG_ROWS, e), BF)] * 3,
        1,
        scratch=(pltpu.VMEM((images_half, e), F32),),
        limit=IMAGE_LIMIT,
    )
    for k, part in enumerate(rest):
        grad_image += lax.ppermute(part, "zh", shift(4, -k - 1)).astype(F32)

    weight_mine, _ = lax.optimization_barrier((weight_mine, rest[0]))
    (gt,) = call(
        text_kernel,
        (weight_other, img_other, weight_mine, img_mine),
        [((16, 2, CAP_DEV, e // 2), BF)],
        limit=TEXT_LIMIT,
    )
    got = lax.all_to_all(gt, ("y", "xl", "xh"), split_axis=0, concat_axis=0, tiled=True)
    gathered = jnp.sum(got.astype(F32), axis=0)
    front = zl == 0
    keep = jnp.where(front, gathered[0], gathered[1])
    give = jnp.where(front, gathered[1], gathered[0])
    grad_text = keep + lax.ppermute(give, "zl", SWAP)

    return (text_part, grad_image, grad_text)


def solution(mesh):
    fine = Mesh(mesh.devices.reshape(SIZES), AXES)
    every = DP + (MP,)
    placed = (
        P(DP, MP),
        P(),
        P(None, MP),
        P(MP, None),
        P(None, MP),
        P(DP, None),
        P(every, None),
        P(every),
        P(),
        P(),
    )
    return jax.shard_map(
        on_device,
        mesh=fine,
        in_specs=placed,
        out_specs=(P(DP, MP), P(every, None), P(DP, MP)),
        check_vma=False,
    )
```

```python
import functools
import jax
import jax.numpy as jnp
from jax import lax
from jax.experimental import pallas as pl
from jax.experimental.pallas import tpu as pltpu
from jax.sharding import Mesh, PartitionSpec as P

CAP_DEV = 32
ROW_TILE = 512
FF_TILE = 1024
IMG_ROWS = 128
GELU_A = 0.7978845608028654
GELU_B = GELU_A * 0.044715
PAD = 128
FIRST_LIMIT = 20
SECOND_LIMIT = 20
IMAGE_LIMIT = 50
TEXT_LIMIT = 50
AXES = ("zh", "zl", "xl", "y", "core", "xh")
SIZES = (4, 2, 2, 4, 2, 2)
DP = ("zh", "zl", "xl", "y", "core")
MP = "xh"
BF = jnp.bfloat16
F32 = jnp.float32
SWAP = [(0, 1), (1, 0)]
LARGE = pl.CostEstimate(flops=10**10, bytes_accessed=1000, transcendentals=0)
SMALL = pl.CostEstimate(flops=1000, bytes_accessed=1000, transcendentals=0)


def dot(a, b):
    return jnp.dot(a, b, preferred_element_type=F32)


def shift(n, k):
    return [(i, (i + k) % n) for i in range(n)]


def mlp_kernel(
    row_tile, ff_tile, low, slot, tokens, arrived, gain, fc_in, fc_out, out, st_out,
    own, other, w_in, w_out, sems
):
    rows, half = own.shape
    ff = w_in.shape[1]
    blocks = [slice(r, r + row_tile) for r in range(0, rows, row_tile)]
    tiles = [slice(j, j + ff_tile) for j in range(0, ff, ff_tile)]
    pairs = []
    for block in blocks:
        pairs.append([(tokens.at[block, :], own.at[block, :])])
        pairs[-1].append((arrived.at[block, :], other.at[block, :]))
    for j, tile in enumerate(tiles):
        pairs.insert(2 * j + 1, [(fc_in.at[:, tile], w_in.at[:, tile])])
    pairs.append([(fc_out, w_out)])
    loads = [
        [pltpu.make_async_copy(a, b, sems.at[i, k]) for k, (a, b) in enumerate(pair)]
        for i, pair in enumerate(pairs)
    ]
    for group in loads:
        for load in group:
            load.start()
    size = 1.0 / (2 * half)
    is_low = low[0] == 1
    pooled = [jnp.zeros((CAP_DEV, ff_tile), F32) for _ in range(ff // ff_tile)]
    states = [jnp.zeros((CAP_DEV, half), F32) for _ in range(2)]
    for i, block in enumerate(blocks):
        for load in loads[2 * i]:
            load.wait()
        captions = lax.broadcasted_iota(jnp.int32, (CAP_DEV, row_tile), 0)
        members = (captions == slot[:, block]).astype(F32).astype(BF)
        mine = own[block, :]
        theirs = other[block, :]
        lo = jnp.where(is_low, mine, theirs)
        hi = jnp.where(is_low, theirs, mine)
        states[0] += dot(members, lo)
        states[1] += dot(members, hi)
        lo = lo.astype(F32)
        hi = hi.astype(F32)
        mean = (jnp.sum(lo, axis=1, keepdims=True) + jnp.sum(hi, axis=1, keepdims=True)) * size
        lo = lo - mean
        hi = hi - mean
        spread = (
            jnp.sum(lo * lo, axis=1, keepdims=True) + jnp.sum(hi * hi, axis=1, keepdims=True)
        ) * size
        inverse = lax.rsqrt(spread + 1e-06)
        normed = jnp.concatenate(
            [
                (lo * inverse * gain[:, :half]).astype(BF),
                (hi * inverse * gain[:, half:]).astype(BF),
            ],
            axis=1,
        )
        for j in range(ff // ff_tile):
            if i == 0:
                loads[2 * j + 1][0].wait()
            pre = dot(normed, w_in[:, j * ff_tile : (j + 1) * ff_tile])
            pre_half = 0.5 * pre
            bend = jnp.tanh(pre * (GELU_A + GELU_B * (pre * pre)))
            hidden = (pre_half + pre_half * bend).astype(BF)
            pooled[j] += dot(members, hidden)
    st_out[:, :half] = states[0]
    st_out[:, half:] = states[1]
    loads[-1][0].wait()
    terms = jnp.zeros((2 * CAP_DEV, w_out.shape[1]), F32)
    for j in range(ff // ff_tile):
        coarse = pooled[j].astype(BF)
        fine = (pooled[j] - coarse.astype(F32)).astype(BF)
        terms += dot(
            jnp.concatenate([coarse, fine], axis=0), w_out[j * ff_tile : (j + 1) * ff_tile, :]
        )
    out[...] = terms[:CAP_DEV] + terms[CAP_DEV:]


def weights_of(scal, columns, texts, img):
    e = texts.shape[1]
    scale, bias = scal[0], scal[1]
    code = img[:, e:].astype(F32)
    marks = (code[:, 0:1] * 64.0 + code[:, 1:2]).astype(jnp.int32)
    logit = lax.dot_general(
        img[:, :e], texts, (((1,), (1,)), ((), ())), preferred_element_type=F32
    )
    logit = scale * logit + bias
    sign = jnp.where(marks == columns[...], 1.0, -1.0).astype(F32)
    return (-scale * sign * jax.nn.sigmoid(-sign * logit)).astype(BF)


def first_kernel(scal, place, columns, emb, exact, img, own_text, texts, weight, gi):
    half = emb.shape[3]
    for g in range(emb.shape[0]):
        lo = emb[g, 0].astype(F32)
        hi = emb[g, 1].astype(F32)
        squares = jnp.sum(lo * lo, axis=1, keepdims=True) + jnp.sum(hi * hi, axis=1, keepdims=True)
        inverse = lax.rsqrt(squares + 1e-06)
        rows = slice(g * CAP_DEV, (g + 1) * CAP_DEV)
        texts[rows, :half] = (lo * inverse).astype(BF)
        texts[rows, half:] = (hi * inverse).astype(BF)
    lo = emb[place[0], 0].astype(F32)
    hi = emb[place[0], 1].astype(F32)
    squares = jnp.sum(lo * lo, axis=1, keepdims=True) + jnp.sum(hi * hi, axis=1, keepdims=True)
    own_text[...] = (exact[...] * lax.rsqrt(squares + 1e-06)).astype(BF)
    w = weights_of(scal, columns, texts[...], img)
    weight[...] = w
    gi[...] = dot(w, texts[...]).astype(BF)


def second_kernel(scal, columns, texts, img, weight):
    weight[...] = weights_of(scal, columns, texts[...], img)


def image_kernel(place, weight, texts, got, own, first, second, third, total):
    total[...] = dot(weight[...], texts[...]) + got[...].astype(F32)
    rows = own.shape[0]
    for k, out in enumerate((own, first, second, third)):
        out[...] = total[k * rows : (k + 1) * rows, :].astype(out.dtype)


def text_kernel(weight_a, img_a, weight_b, img_b, out):
    half = out.shape[3]
    e = 2 * half
    turned = (((0,), (0,)), ((), ()))
    gt = lax.dot_general(weight_a[...], img_a[:, :e], turned, preferred_element_type=F32)
    gt += lax.dot_general(weight_b[...], img_b[:, :e], turned, preferred_element_type=F32)
    groups = out.shape[0] // 2
    for z in range(2):
        for g in range(groups):
            row = (z * groups + g) * CAP_DEV
            for h in range(2):
                out[2 * g + h, z] = gt[row : row + CAP_DEV, h * half : (h + 1) * half].astype(BF)


def call(kernel, args, outs, scalars=0, far=(), free=(), scratch=(), cost=SMALL, limit=20):
    in_specs = [
        pl.BlockSpec(
            memory_space=pltpu.SMEM
            if i < scalars
            else pltpu.HBM if i in far else pl.ANY if i in free else pltpu.VMEM
        )
        for i in range(len(args))
    ]
    return pl.pallas_call(
        kernel,
        in_specs=in_specs,
        out_specs=[pl.BlockSpec(memory_space=pltpu.VMEM) for _ in outs],
        out_shape=[jax.ShapeDtypeStruct(shape, dtype) for shape, dtype in outs],
        scratch_shapes=list(scratch),
        compiler_params=pltpu.CompilerParams(vmem_limit_bytes=limit << 20),
        cost_estimate=cost,
    )(*args)


def on_device(
    tokens, norm_gain, fc_in, fc_out, projection, slots, images, labels, logit_scale, logit_bias
):
    zh, core, xh = (lax.axis_index(a) for a in ("zh", "core", "xh"))
    low = xh == 0

    other = lax.ppermute(tokens, MP, SWAP)

    imgs = images.astype(F32)
    img = (imgs * lax.rsqrt(jnp.sum(imgs * imgs, axis=1, keepdims=True) + 1e-06)).astype(BF)
    code = jnp.stack([labels // 64, labels % 64], axis=1).astype(F32).astype(BF)
    img = jnp.concatenate([img, jnp.pad(code, ((0, 0), (0, PAD - 2)))], axis=1)
    img_mine = jnp.concatenate(
        [img] + [lax.ppermute(img, "zh", shift(4, k)) for k in (1, 2, 3)], axis=0
    )

    members = slots[0][None, :] == jnp.arange(CAP_DEV, dtype=jnp.int32)[:, None]
    counts = jnp.sum(members.astype(F32), axis=1)
    flag = low.astype(jnp.int32).reshape(1)
    partial_out, states = call(
        functools.partial(mlp_kernel, ROW_TILE, FF_TILE),
        (flag, slots, tokens, other, norm_gain[None, :], fc_in, fc_out),
        [((CAP_DEV, fc_out.shape[1]), F32), ((CAP_DEV, fc_in.shape[0]), F32)],
        1,
        far=(2, 5, 6),
        free=(3,),
        scratch=(
            pltpu.VMEM(tokens.shape, BF),
            pltpu.VMEM(tokens.shape, BF),
            pltpu.VMEM(fc_in.shape, BF),
            pltpu.VMEM(fc_out.shape, BF),
            pltpu.SemaphoreType.DMA((5, 2)),
        ),
        cost=LARGE,
        limit=54,
    )
    summed = partial_out + lax.ppermute(partial_out, MP, SWAP)
    summed, img_mine = lax.optimization_barrier((summed, img_mine))
    pooled = ((states + summed) / counts[:, None]).astype(BF)
    emb = dot(pooled, projection)
    sent = jnp.broadcast_to(emb.astype(BF)[None], (32,) + emb.shape)

    group = ("zl", "y", "xl", "xh")
    embs = lax.all_to_all(sent, group, split_axis=0, concat_axis=0, tiled=True)
    embs = embs.reshape((16, 2) + emb.shape)
    img_sent, _ = lax.optimization_barrier((img_mine, emb))
    img_other = lax.ppermute(img_sent, "core", SWAP)

    zl_i, y_i, xl_i, cap_i = (
        lax.broadcasted_iota(jnp.int32, (2, 4, 2, CAP_DEV), d) for d in range(4)
    )
    columns = (((((zh * 2 + zl_i) * 2 + xl_i) * 4 + y_i) * 2 + core) * CAP_DEV + cap_i).reshape(1, -1)
    scal = jnp.concatenate([logit_scale, logit_bias])
    n, e = 16 * CAP_DEV, fc_in.shape[0]
    images_half = img_mine.shape[0]
    zl, y, xl = (lax.axis_index(a) for a in ("zl", "y", "xl"))
    place = ((zl * 4 + y) * 2 + xl).astype(jnp.int32).reshape(1)
    text_part, texts, weight_other, gi_send = call(
        first_kernel,
        (scal, place, columns, embs, emb, img_other),
        [(emb.shape, BF), ((n, e), BF), ((images_half, n), BF), ((images_half, e), BF)],
        2,
        limit=FIRST_LIMIT,
    )
    gi_got = lax.ppermute(gi_send, "core", SWAP)
    (weight_mine,) = call(
        second_kernel, (scal, columns, texts, img_mine), [((images_half, n), BF)], 1,
        limit=SECOND_LIMIT,
    )

    gi_got, weight_mine = lax.optimization_barrier((gi_got, weight_mine))
    grad_image, *rest = call(
        image_kernel,
        (zh.astype(jnp.int32).reshape(1), weight_mine, texts, gi_got),
        [((IMG_ROWS, e), F32)] + [((IMG_ROWS, e), BF)] * 3,
        1,
        scratch=(pltpu.VMEM((images_half, e), F32),),
        limit=IMAGE_LIMIT,
    )
    for k, part in enumerate(rest):
        grad_image += lax.ppermute(part, "zh", shift(4, -k - 1)).astype(F32)

    weight_mine, _ = lax.optimization_barrier((weight_mine, rest[0]))
    (gt,) = call(
        text_kernel,
        (weight_other, img_other, weight_mine, img_mine),
        [((16, 2, CAP_DEV, e // 2), BF)],
        limit=TEXT_LIMIT,
    )
    got = lax.all_to_all(gt, ("y", "xl", "xh"), split_axis=0, concat_axis=0, tiled=True)
    gathered = jnp.sum(got.astype(F32), axis=0)
    front = zl == 0
    keep = jnp.where(front, gathered[0], gathered[1])
    give = jnp.where(front, gathered[1], gathered[0])
    grad_text = keep + lax.ppermute(give, "zl", SWAP)

    return (text_part, grad_image, grad_text)


def solution(mesh):
    fine = Mesh(mesh.devices.reshape(SIZES), AXES)
    every = DP + (MP,)
    placed = (
        P(DP, MP),
        P(),
        P(None, MP),
        P(MP, None),
        P(None, MP),
        P(DP, None),
        P(every, None),
        P(every),
        P(),
        P(),
    )
    return jax.shard_map(
        on_device,
        mesh=fine,
        in_specs=placed,
        out_specs=(P(DP, MP), P(every, None), P(DP, MP)),
        check_vma=False,
    )
```

```python
import functools
import jax
import jax.numpy as jnp
from jax import lax
from jax.experimental import pallas as pl
from jax.experimental.pallas import tpu as pltpu
from jax.sharding import Mesh, PartitionSpec as P

CAP_DEV = 32
ROW_TILE = 512
FF_TILE = 1024
IMG_ROWS = 128
GELU_A = 0.7978845608028654
GELU_B = GELU_A * 0.044715
PAD = 128
FIRST_LIMIT = 20
SECOND_LIMIT = 20
IMAGE_LIMIT = 20
TEXT_LIMIT = 50
AXES = ("zh", "zl", "xl", "y", "core", "xh")
SIZES = (4, 2, 2, 4, 2, 2)
DP = ("zh", "zl", "xl", "y", "core")
MP = "xh"
BF = jnp.bfloat16
F32 = jnp.float32
SWAP = [(0, 1), (1, 0)]
LARGE = pl.CostEstimate(flops=10**10, bytes_accessed=1000, transcendentals=0)
SMALL = pl.CostEstimate(flops=1000, bytes_accessed=1000, transcendentals=0)


def dot(a, b):
    return jnp.dot(a, b, preferred_element_type=F32)


def shift(n, k):
    return [(i, (i + k) % n) for i in range(n)]


def mlp_kernel(
    row_tile, ff_tile, low, slot, tokens, arrived, gain, fc_in, fc_out, out, st_out,
    own, other, w_in, w_out, sems
):
    rows, half = own.shape
    ff = w_in.shape[1]
    blocks = [slice(r, r + row_tile) for r in range(0, rows, row_tile)]
    tiles = [slice(j, j + ff_tile) for j in range(0, ff, ff_tile)]
    pairs = []
    for block in blocks:
        pairs.append([(tokens.at[block, :], own.at[block, :])])
        pairs[-1].append((arrived.at[block, :], other.at[block, :]))
    for j, tile in enumerate(tiles):
        pairs.insert(2 * j + 1, [(fc_in.at[:, tile], w_in.at[:, tile])])
    pairs.append([(fc_out, w_out)])
    loads = [
        [pltpu.make_async_copy(a, b, sems.at[i, k]) for k, (a, b) in enumerate(pair)]
        for i, pair in enumerate(pairs)
    ]
    for group in loads:
        for load in group:
            load.start()
    size = 1.0 / (2 * half)
    is_low = low[0] == 1
    pooled = [jnp.zeros((CAP_DEV, ff_tile), F32) for _ in range(ff // ff_tile)]
    states = [jnp.zeros((CAP_DEV, half), F32) for _ in range(2)]
    for i, block in enumerate(blocks):
        for load in loads[2 * i]:
            load.wait()
        captions = lax.broadcasted_iota(jnp.int32, (CAP_DEV, row_tile), 0)
        members = (captions == slot[:, block]).astype(F32).astype(BF)
        mine = own[block, :]
        theirs = other[block, :]
        lo = jnp.where(is_low, mine, theirs)
        hi = jnp.where(is_low, theirs, mine)
        states[0] += dot(members, lo)
        states[1] += dot(members, hi)
        lo = lo.astype(F32)
        hi = hi.astype(F32)
        mean = (jnp.sum(lo, axis=1, keepdims=True) + jnp.sum(hi, axis=1, keepdims=True)) * size
        lo = lo - mean
        hi = hi - mean
        spread = (
            jnp.sum(lo * lo, axis=1, keepdims=True) + jnp.sum(hi * hi, axis=1, keepdims=True)
        ) * size
        inverse = lax.rsqrt(spread + 1e-06)
        normed = jnp.concatenate(
            [
                (lo * inverse * gain[:, :half]).astype(BF),
                (hi * inverse * gain[:, half:]).astype(BF),
            ],
            axis=1,
        )
        for j in range(ff // ff_tile):
            if i == 0:
                loads[2 * j + 1][0].wait()
            pre = dot(normed, w_in[:, j * ff_tile : (j + 1) * ff_tile])
            pre_half = 0.5 * pre
            bend = jnp.tanh(pre * (GELU_A + GELU_B * (pre * pre)))
            hidden = (pre_half + pre_half * bend).astype(BF)
            pooled[j] += dot(members, hidden)
    st_out[:, :half] = states[0]
    st_out[:, half:] = states[1]
    loads[-1][0].wait()
    terms = jnp.zeros((2 * CAP_DEV, w_out.shape[1]), F32)
    for j in range(ff // ff_tile):
        coarse = pooled[j].astype(BF)
        fine = (pooled[j] - coarse.astype(F32)).astype(BF)
        terms += dot(
            jnp.concatenate([coarse, fine], axis=0), w_out[j * ff_tile : (j + 1) * ff_tile, :]
        )
    out[...] = terms[:CAP_DEV] + terms[CAP_DEV:]


def weights_of(scal, columns, texts, img):
    e = texts.shape[1]
    scale, bias = scal[0], scal[1]
    code = img[:, e:].astype(F32)
    marks = (code[:, 0:1] * 64.0 + code[:, 1:2]).astype(jnp.int32)
    logit = lax.dot_general(
        img[:, :e], texts, (((1,), (1,)), ((), ())), preferred_element_type=F32
    )
    logit = scale * logit + bias
    sign = jnp.where(marks == columns[...], 1.0, -1.0).astype(F32)
    return (-scale * sign * jax.nn.sigmoid(-sign * logit)).astype(BF)


def first_kernel(scal, place, columns, emb, exact, img, own_text, texts, weight, gi):
    half = emb.shape[3]
    for g in range(emb.shape[0]):
        lo = emb[g, 0].astype(F32)
        hi = emb[g, 1].astype(F32)
        squares = jnp.sum(lo * lo, axis=1, keepdims=True) + jnp.sum(hi * hi, axis=1, keepdims=True)
        inverse = lax.rsqrt(squares + 1e-06)
        rows = slice(g * CAP_DEV, (g + 1) * CAP_DEV)
        texts[rows, :half] = (lo * inverse).astype(BF)
        texts[rows, half:] = (hi * inverse).astype(BF)
    lo = emb[place[0], 0].astype(F32)
    hi = emb[place[0], 1].astype(F32)
    squares = jnp.sum(lo * lo, axis=1, keepdims=True) + jnp.sum(hi * hi, axis=1, keepdims=True)
    own_text[...] = (exact[...] * lax.rsqrt(squares + 1e-06)).astype(BF)
    w = weights_of(scal, columns, texts[...], img)
    weight[...] = w
    gi[...] = dot(w, texts[...]).astype(BF)


def second_kernel(scal, columns, texts, img, weight):
    weight[...] = weights_of(scal, columns, texts[...], img)


def image_kernel(place, weight, texts, got, own, first, second, third, total):
    total[...] = dot(weight[...], texts[...]) + got[...].astype(F32)
    rows = own.shape[0]
    for k, out in enumerate((own, first, second, third)):
        slot = lax.rem(place[0] + (4 - k), 4)
        out[...] = total[pl.ds(pl.multiple_of(slot * rows, rows), rows), :].astype(out.dtype)


def text_kernel(weight_a, img_a, weight_b, img_b, out):
    half = out.shape[3]
    e = 2 * half
    turned = (((0,), (0,)), ((), ()))
    gt = lax.dot_general(weight_a[...], img_a[:, :e], turned, preferred_element_type=F32)
    gt += lax.dot_general(weight_b[...], img_b[:, :e], turned, preferred_element_type=F32)
    groups = out.shape[0] // 2
    for z in range(2):
        for g in range(groups):
            row = (z * groups + g) * CAP_DEV
            for h in range(2):
                out[2 * g + h, z] = gt[row : row + CAP_DEV, h * half : (h + 1) * half].astype(BF)


def call(kernel, args, outs, scalars=0, far=(), free=(), scratch=(), cost=SMALL, limit=20):
    in_specs = [
        pl.BlockSpec(
            memory_space=pltpu.SMEM
            if i < scalars
            else pltpu.HBM if i in far else pl.ANY if i in free else pltpu.VMEM
        )
        for i in range(len(args))
    ]
    return pl.pallas_call(
        kernel,
        in_specs=in_specs,
        out_specs=[pl.BlockSpec(memory_space=pltpu.VMEM) for _ in outs],
        out_shape=[jax.ShapeDtypeStruct(shape, dtype) for shape, dtype in outs],
        scratch_shapes=list(scratch),
        compiler_params=pltpu.CompilerParams(vmem_limit_bytes=limit << 20),
        cost_estimate=cost,
    )(*args)


def on_device(
    tokens, norm_gain, fc_in, fc_out, projection, slots, images, labels, logit_scale, logit_bias
):
    zh, core, xh = (lax.axis_index(a) for a in ("zh", "core", "xh"))
    low = xh == 0

    other = lax.ppermute(tokens, MP, SWAP)

    imgs = images.astype(F32)
    img = (imgs * lax.rsqrt(jnp.sum(imgs * imgs, axis=1, keepdims=True) + 1e-06)).astype(BF)
    code = jnp.stack([labels // 64, labels % 64], axis=1).astype(F32).astype(BF)
    img = jnp.concatenate([img, jnp.pad(code, ((0, 0), (0, PAD - 2)))], axis=1)
    img_mine = lax.all_to_all(
        jnp.broadcast_to(img[None], (4,) + img.shape), "zh", split_axis=0, concat_axis=0, tiled=True
    ).reshape(4 * IMG_ROWS, -1)

    members = slots[0][None, :] == jnp.arange(CAP_DEV, dtype=jnp.int32)[:, None]
    counts = jnp.sum(members.astype(F32), axis=1)
    flag = low.astype(jnp.int32).reshape(1)
    partial_out, states = call(
        functools.partial(mlp_kernel, ROW_TILE, FF_TILE),
        (flag, slots, tokens, other, norm_gain[None, :], fc_in, fc_out),
        [((CAP_DEV, fc_out.shape[1]), F32), ((CAP_DEV, fc_in.shape[0]), F32)],
        1,
        far=(2, 5, 6),
        free=(3,),
        scratch=(
            pltpu.VMEM(tokens.shape, BF),
            pltpu.VMEM(tokens.shape, BF),
            pltpu.VMEM(fc_in.shape, BF),
            pltpu.VMEM(fc_out.shape, BF),
            pltpu.SemaphoreType.DMA((5, 2)),
        ),
        cost=LARGE,
        limit=48,
    )
    summed = partial_out + lax.ppermute(partial_out, MP, SWAP)
    pooled = ((states + summed) / counts[:, None]).astype(BF)
    emb = dot(pooled, projection)
    sent = jnp.broadcast_to(emb.astype(BF)[None], (32,) + emb.shape)

    group = ("zl", "y", "xl", "xh")
    embs = lax.all_to_all(sent, group, split_axis=0, concat_axis=0, tiled=True)
    embs = embs.reshape((16, 2) + emb.shape)
    img_sent, _ = lax.optimization_barrier((img_mine, emb))
    img_other = lax.ppermute(img_sent, "core", SWAP)

    zl_i, y_i, xl_i, cap_i = (
        lax.broadcasted_iota(jnp.int32, (2, 4, 2, CAP_DEV), d) for d in range(4)
    )
    columns = (((((zh * 2 + zl_i) * 2 + xl_i) * 4 + y_i) * 2 + core) * CAP_DEV + cap_i).reshape(1, -1)
    scal = jnp.concatenate([logit_scale, logit_bias])
    n, e = 16 * CAP_DEV, fc_in.shape[0]
    images_half = img_mine.shape[0]
    zl, y, xl = (lax.axis_index(a) for a in ("zl", "y", "xl"))
    place = ((zl * 4 + y) * 2 + xl).astype(jnp.int32).reshape(1)
    text_part, texts, weight_other, gi_send = call(
        first_kernel,
        (scal, place, columns, embs, emb, img_other),
        [(emb.shape, BF), ((n, e), BF), ((images_half, n), BF), ((images_half, e), BF)],
        2,
        limit=FIRST_LIMIT,
    )
    gi_got = lax.ppermute(gi_send, "core", SWAP)
    (weight_mine,) = call(
        second_kernel, (scal, columns, texts, img_mine), [((images_half, n), BF)], 1,
        limit=SECOND_LIMIT,
    )

    gi_got, weight_mine = lax.optimization_barrier((gi_got, weight_mine))
    grad_image, *rest = call(
        image_kernel,
        (zh.astype(jnp.int32).reshape(1), weight_mine, texts, gi_got),
        [((IMG_ROWS, e), F32)] + [((IMG_ROWS, e), BF)] * 3,
        1,
        scratch=(pltpu.VMEM((images_half, e), F32),),
        limit=IMAGE_LIMIT,
    )
    for k, part in enumerate(rest):
        grad_image += lax.ppermute(part, "zh", shift(4, -k - 1)).astype(F32)

    weight_mine, _ = lax.optimization_barrier((weight_mine, rest[0]))
    (gt,) = call(
        text_kernel,
        (weight_other, img_other, weight_mine, img_mine),
        [((16, 2, CAP_DEV, e // 2), BF)],
        limit=TEXT_LIMIT,
    )
    got = lax.all_to_all(gt, ("y", "xl", "xh"), split_axis=0, concat_axis=0, tiled=True)
    gathered = jnp.sum(got.astype(F32), axis=0)
    front = zl == 0
    keep = jnp.where(front, gathered[0], gathered[1])
    give = jnp.where(front, gathered[1], gathered[0])
    grad_text = keep + lax.ppermute(give, "zl", SWAP)

    return (text_part, grad_image, grad_text)


def solution(mesh):
    fine = Mesh(mesh.devices.reshape(SIZES), AXES)
    every = DP + (MP,)
    placed = (
        P(DP, MP),
        P(),
        P(None, MP),
        P(MP, None),
        P(None, MP),
        P(DP, None),
        P(every, None),
        P(every),
        P(),
        P(),
    )
    return jax.shard_map(
        on_device,
        mesh=fine,
        in_specs=placed,
        out_specs=(P(DP, MP), P(every, None), P(DP, MP)),
        check_vma=False,
    )
```

```python
import functools
import jax
import jax.numpy as jnp
from jax import lax
from jax.experimental import pallas as pl
from jax.experimental.pallas import tpu as pltpu
from jax.sharding import Mesh, PartitionSpec as P

CAP_DEV = 32
ROW_TILE = 512
FF_TILE = 1024
IMG_ROWS = 128
GELU_A = 0.7978845608028654
GELU_B = GELU_A * 0.044715
PAD = 128
FIRST_LIMIT = 20
SECOND_LIMIT = 20
IMAGE_LIMIT = 20
TEXT_LIMIT = 50
AXES = ("zh", "zl", "xl", "y", "core", "xh")
SIZES = (4, 2, 2, 4, 2, 2)
DP = ("zh", "zl", "xl", "y", "core")
MP = "xh"
BF = jnp.bfloat16
F32 = jnp.float32
SWAP = [(0, 1), (1, 0)]
LARGE = pl.CostEstimate(flops=10**10, bytes_accessed=1000, transcendentals=0)
SMALL = pl.CostEstimate(flops=1000, bytes_accessed=1000, transcendentals=0)


def dot(a, b):
    return jnp.dot(a, b, preferred_element_type=F32)


def shift(n, k):
    return [(i, (i + k) % n) for i in range(n)]


def prepare_kernel(images, labels, out):
    e = images.shape[1]
    rows = images[...].astype(F32)
    img = (rows * lax.rsqrt(jnp.sum(rows * rows, axis=1, keepdims=True) + 1e-06)).astype(BF)
    place = lax.broadcasted_iota(jnp.int32, (images.shape[0], PAD), 1)
    mark = labels[...]
    code = jnp.where(place == 0, mark >> 6, jnp.where(place == 1, mark & 63, 0))
    code = code.astype(F32).astype(BF)
    for i in range(out.shape[0]):
        out[i, :, :e] = img
        out[i, :, e:] = code


def mlp_kernel(
    row_tile, ff_tile, low, slot, tokens, arrived, gain, fc_in, fc_out, out, st_out,
    own, other, w_in, w_out, sems
):
    rows, half = own.shape
    ff = w_in.shape[1]
    blocks = [slice(r, r + row_tile) for r in range(0, rows, row_tile)]
    tiles = [slice(j, j + ff_tile) for j in range(0, ff, ff_tile)]
    pairs = []
    for block in blocks:
        pairs.append([(tokens.at[block, :], own.at[block, :])])
        pairs[-1].append((arrived.at[block, :], other.at[block, :]))
    for j, tile in enumerate(tiles):
        pairs.insert(2 * j + 1, [(fc_in.at[:, tile], w_in.at[:, tile])])
    pairs.append([(fc_out, w_out)])
    loads = [
        [pltpu.make_async_copy(a, b, sems.at[i, k]) for k, (a, b) in enumerate(pair)]
        for i, pair in enumerate(pairs)
    ]
    for group in loads:
        for load in group:
            load.start()
    size = 1.0 / (2 * half)
    is_low = low[0] == 1
    pooled = [jnp.zeros((CAP_DEV, ff_tile), F32) for _ in range(ff // ff_tile)]
    states = [jnp.zeros((CAP_DEV, half), F32) for _ in range(2)]
    for i, block in enumerate(blocks):
        for load in loads[2 * i]:
            load.wait()
        captions = lax.broadcasted_iota(jnp.int32, (CAP_DEV, row_tile), 0)
        members = (captions == slot[:, block]).astype(F32).astype(BF)
        mine = own[block, :]
        theirs = other[block, :]
        lo = jnp.where(is_low, mine, theirs)
        hi = jnp.where(is_low, theirs, mine)
        states[0] += dot(members, lo)
        states[1] += dot(members, hi)
        lo = lo.astype(F32)
        hi = hi.astype(F32)
        mean = (jnp.sum(lo, axis=1, keepdims=True) + jnp.sum(hi, axis=1, keepdims=True)) * size
        lo = lo - mean
        hi = hi - mean
        spread = (
            jnp.sum(lo * lo, axis=1, keepdims=True) + jnp.sum(hi * hi, axis=1, keepdims=True)
        ) * size
        inverse = lax.rsqrt(spread + 1e-06)
        normed = jnp.concatenate(
            [
                (lo * inverse * gain[:, :half]).astype(BF),
                (hi * inverse * gain[:, half:]).astype(BF),
            ],
            axis=1,
        )
        for j in range(ff // ff_tile):
            if i == 0:
                loads[2 * j + 1][0].wait()
            pre = dot(normed, w_in[:, j * ff_tile : (j + 1) * ff_tile])
            pre_half = 0.5 * pre
            bend = jnp.tanh(pre * (GELU_A + GELU_B * (pre * pre)))
            hidden = (pre_half + pre_half * bend).astype(BF)
            pooled[j] += dot(members, hidden)
    st_out[:, :half] = states[0]
    st_out[:, half:] = states[1]
    loads[-1][0].wait()
    terms = jnp.zeros((2 * CAP_DEV, w_out.shape[1]), F32)
    for j in range(ff // ff_tile):
        coarse = pooled[j].astype(BF)
        fine = (pooled[j] - coarse.astype(F32)).astype(BF)
        terms += dot(
            jnp.concatenate([coarse, fine], axis=0), w_out[j * ff_tile : (j + 1) * ff_tile, :]
        )
    out[...] = terms[:CAP_DEV] + terms[CAP_DEV:]


def weights_of(scal, columns, texts, img):
    e = texts.shape[1]
    scale, bias = scal[0], scal[1]
    code = img[:, e:].astype(F32)
    marks = (code[:, 0:1] * 64.0 + code[:, 1:2]).astype(jnp.int32)
    logit = lax.dot_general(
        img[:, :e], texts, (((1,), (1,)), ((), ())), preferred_element_type=F32
    )
    logit = scale * logit + bias
    sign = jnp.where(marks == columns[...], 1.0, -1.0).astype(F32)
    return (-scale * sign * jax.nn.sigmoid(-sign * logit)).astype(BF)


def first_kernel(scal, place, columns, emb, exact, img, own_text, texts, weight, gi):
    half = emb.shape[3]
    for g in range(emb.shape[0]):
        lo = emb[g, 0].astype(F32)
        hi = emb[g, 1].astype(F32)
        squares = jnp.sum(lo * lo, axis=1, keepdims=True) + jnp.sum(hi * hi, axis=1, keepdims=True)
        inverse = lax.rsqrt(squares + 1e-06)
        rows = slice(g * CAP_DEV, (g + 1) * CAP_DEV)
        texts[rows, :half] = (lo * inverse).astype(BF)
        texts[rows, half:] = (hi * inverse).astype(BF)
    lo = emb[place[0], 0].astype(F32)
    hi = emb[place[0], 1].astype(F32)
    squares = jnp.sum(lo * lo, axis=1, keepdims=True) + jnp.sum(hi * hi, axis=1, keepdims=True)
    own_text[...] = (exact[...] * lax.rsqrt(squares + 1e-06)).astype(BF)
    w = weights_of(scal, columns, texts[...], img)
    weight[...] = w
    gi[...] = dot(w, texts[...]).astype(BF)


def second_kernel(scal, columns, texts, img, weight):
    weight[...] = weights_of(scal, columns, texts[...], img)


def image_kernel(place, weight, texts, got, own, first, second, third, total):
    total[...] = dot(weight[...], texts[...]) + got[...].astype(F32)
    rows = own.shape[0]
    for k, out in enumerate((own, first, second, third)):
        slot = lax.rem(place[0] + (4 - k), 4)
        out[...] = total[pl.ds(pl.multiple_of(slot * rows, rows), rows), :].astype(out.dtype)


def text_kernel(weight_a, img_a, weight_b, img_b, out):
    half = out.shape[3]
    e = 2 * half
    turned = (((0,), (0,)), ((), ()))
    gt = lax.dot_general(weight_a[...], img_a[:, :e], turned, preferred_element_type=F32)
    gt += lax.dot_general(weight_b[...], img_b[:, :e], turned, preferred_element_type=F32)
    groups = out.shape[0] // 2
    for z in range(2):
        for g in range(groups):
            row = (z * groups + g) * CAP_DEV
            for h in range(2):
                out[2 * g + h, z] = gt[row : row + CAP_DEV, h * half : (h + 1) * half].astype(BF)


def call(kernel, args, outs, scalars=0, far=(), free=(), scratch=(), cost=SMALL, limit=20):
    in_specs = [
        pl.BlockSpec(
            memory_space=pltpu.SMEM
            if i < scalars
            else pltpu.HBM if i in far else pl.ANY if i in free else pltpu.VMEM
        )
        for i in range(len(args))
    ]
    return pl.pallas_call(
        kernel,
        in_specs=in_specs,
        out_specs=[pl.BlockSpec(memory_space=pltpu.VMEM) for _ in outs],
        out_shape=[jax.ShapeDtypeStruct(shape, dtype) for shape, dtype in outs],
        scratch_shapes=list(scratch),
        compiler_params=pltpu.CompilerParams(vmem_limit_bytes=limit << 20),
        cost_estimate=cost,
    )(*args)


def on_device(
    tokens, norm_gain, fc_in, fc_out, projection, slots, images, labels, logit_scale, logit_bias
):
    zh, core, xh = (lax.axis_index(a) for a in ("zh", "core", "xh"))
    low = xh == 0

    other = lax.ppermute(tokens, MP, SWAP)

    (img_sent,) = call(
        prepare_kernel,
        (images, labels[:, None]),
        [((4,) + (images.shape[0], images.shape[1] + PAD), BF)],
    )
    img_mine = lax.all_to_all(img_sent, "zh", split_axis=0, concat_axis=0, tiled=True)
    img_mine = img_mine.reshape(4 * IMG_ROWS, -1)

    members = slots[0][None, :] == jnp.arange(CAP_DEV, dtype=jnp.int32)[:, None]
    counts = jnp.sum(members.astype(F32), axis=1)
    flag = low.astype(jnp.int32).reshape(1)
    partial_out, states = call(
        functools.partial(mlp_kernel, ROW_TILE, FF_TILE),
        (flag, slots, tokens, other, norm_gain[None, :], fc_in, fc_out),
        [((CAP_DEV, fc_out.shape[1]), F32), ((CAP_DEV, fc_in.shape[0]), F32)],
        1,
        far=(2, 5, 6),
        free=(3,),
        scratch=(
            pltpu.VMEM(tokens.shape, BF),
            pltpu.VMEM(tokens.shape, BF),
            pltpu.VMEM(fc_in.shape, BF),
            pltpu.VMEM(fc_out.shape, BF),
            pltpu.SemaphoreType.DMA((5, 2)),
        ),
        cost=LARGE,
        limit=48,
    )
    summed = partial_out + lax.ppermute(partial_out, MP, SWAP)
    pooled = ((states + summed) / counts[:, None]).astype(BF)
    emb = dot(pooled, projection)
    sent = jnp.broadcast_to(emb.astype(BF)[None], (32,) + emb.shape)

    group = ("zl", "y", "xl", "xh")
    embs = lax.all_to_all(sent, group, split_axis=0, concat_axis=0, tiled=True)
    embs = embs.reshape((16, 2) + emb.shape)
    img_sent, _ = lax.optimization_barrier((img_mine, emb))
    img_other = lax.ppermute(img_sent, "core", SWAP)

    zl_i, y_i, xl_i, cap_i = (
        lax.broadcasted_iota(jnp.int32, (2, 4, 2, CAP_DEV), d) for d in range(4)
    )
    columns = (((((zh * 2 + zl_i) * 2 + xl_i) * 4 + y_i) * 2 + core) * CAP_DEV + cap_i).reshape(1, -1)
    scal = jnp.concatenate([logit_scale, logit_bias])
    n, e = 16 * CAP_DEV, fc_in.shape[0]
    images_half = img_mine.shape[0]
    zl, y, xl = (lax.axis_index(a) for a in ("zl", "y", "xl"))
    place = ((zl * 4 + y) * 2 + xl).astype(jnp.int32).reshape(1)
    text_part, texts, weight_other, gi_send = call(
        first_kernel,
        (scal, place, columns, embs, emb, img_other),
        [(emb.shape, BF), ((n, e), BF), ((images_half, n), BF), ((images_half, e), BF)],
        2,
        limit=FIRST_LIMIT,
    )
    gi_got = lax.ppermute(gi_send, "core", SWAP)
    (weight_mine,) = call(
        second_kernel, (scal, columns, texts, img_mine), [((images_half, n), BF)], 1,
        limit=SECOND_LIMIT,
    )

    gi_got, weight_mine = lax.optimization_barrier((gi_got, weight_mine))
    grad_image, *rest = call(
        image_kernel,
        (zh.astype(jnp.int32).reshape(1), weight_mine, texts, gi_got),
        [((IMG_ROWS, e), F32)] + [((IMG_ROWS, e), BF)] * 3,
        1,
        scratch=(pltpu.VMEM((images_half, e), F32),),
        limit=IMAGE_LIMIT,
    )
    for k, part in enumerate(rest):
        grad_image += lax.ppermute(part, "zh", shift(4, -k - 1)).astype(F32)

    weight_mine, _ = lax.optimization_barrier((weight_mine, rest[0]))
    (gt,) = call(
        text_kernel,
        (weight_other, img_other, weight_mine, img_mine),
        [((16, 2, CAP_DEV, e // 2), BF)],
        limit=TEXT_LIMIT,
    )
    got = lax.all_to_all(gt, ("y", "xl", "xh"), split_axis=0, concat_axis=0, tiled=True)
    gathered = jnp.sum(got.astype(F32), axis=0)
    front = zl == 0
    keep = jnp.where(front, gathered[0], gathered[1])
    give = jnp.where(front, gathered[1], gathered[0])
    grad_text = keep + lax.ppermute(give, "zl", SWAP)

    return (text_part, grad_image, grad_text)


def solution(mesh):
    fine = Mesh(mesh.devices.reshape(SIZES), AXES)
    every = DP + (MP,)
    placed = (
        P(DP, MP),
        P(),
        P(None, MP),
        P(MP, None),
        P(None, MP),
        P(DP, None),
        P(every, None),
        P(every),
        P(),
        P(),
    )
    return jax.shard_map(
        on_device,
        mesh=fine,
        in_specs=placed,
        out_specs=(P(DP, MP), P(every, None), P(DP, MP)),
        check_vma=False,
    )
```
